32 devices in a mesh: batch: 8 (over z, x), seq: 4 (over y, core).
Axes of the slice: x: 2, y: 2, z: 4, core: 2. Of those that a mesh axis runs over, the one named last changes fastest.
Arguments:
- tokens: bfloat16 [32, 512, 768], P('batch', 'seq'), may hold values from -6 to 6
- lengths: int32 [32, 8], P('batch'), may hold values from 1 to 512, as said below
- positives: int32 [128], replicated, may hold values from 0 to 127, each once
- qkv_weight: bfloat16 [2, 768, 2304], replicated, may hold values from -0.21875 to 0.21875
- attn_bias: float32 [2, 3, 768], replicated, may hold values from -3 to 3
- out_weight: bfloat16 [2, 768, 768], replicated, may hold values from -0.875 to 0.875
- ffn_in: bfloat16 [2, 768, 3072], replicated, may hold values from -0.21875 to 0.21875
- ffn_in_bias: float32 [2, 3072], replicated, may hold values from -3 to 3
- ffn_out: bfloat16 [2, 3072, 768], replicated, may hold values from -0.109375 to 0.109375
- ffn_out_bias: float32 [2, 768], replicated, may hold values from -2 to 2
- norm_gain: float32 [2, 2, 768], replicated, may hold values from 0.5 to 1.5
- norm_bias: float32 [2, 2, 768], replicated, may hold values from -1.5 to 1.5
- cotangent: bfloat16 [32, 512, 768], P('batch', 'seq'), may hold values from -6 to 6
Outputs:
- layer_output: bfloat16 [32, 512, 768], P('batch', 'seq')
- input_grad: float32 [32, 512, 768], P('batch', 'seq')
- contrast_loss: float32 [], replicated
- qkv_weight_grad: float32 [2, 768, 2304], P(None, 'batch')
- attn_bias_grad: float32 [2, 3, 768], P(None, None, 'batch')
- out_weight_grad: float32 [2, 768, 768], P(None, 'batch')
- ffn_in_grad: float32 [2, 768, 3072], P(None, 'batch')
- ffn_in_bias_grad: float32 [2, 3072], P(None, 'batch')
- ffn_out_grad: float32 [2, 3072, 768], P(None, 'batch')
- ffn_out_bias_grad: float32 [2, 768], P(None, 'batch')
- norm_gain_grad: float32 [2, 2, 768], P(None, None, 'batch')
- norm_bias_grad: float32 [2, 2, 768], P(None, None, 'batch')
The draws below stay inside these ranges and needn't reach their ends.
Inputs may be any that keep to these rules, and one draw needn't show every extreme that they name: Each row's 8 lengths sum to 512. In a row of queries (even rows) all but one of them are at most 18. `positives`: every passage is the positive of exactly one query.
All inputs are finite; a program needn't handle non-finite values.
Results may differ from the reference program's by a relative error of at most 0.018.
Values may be sent and summed in bfloat16 or wider, within the bound.
No kernel may reach another device: no remote copies, remote signals or barrier semaphores. Data moves between devices by JAX's collectives and lax.ppermute only.
A program may use at most 256 MiB of HBM per device.

```python
import math
import jax
import jax.numpy as jnp
from jax import lax

D = 768
HEADS = 12
HEAD_DIM = 64
FF = 3072
L = 512
LAYERS = 2
SEGS = 8
SHORT_MOST = 18
ROWS = 32
NQ = 128


def draw_lengths(key, part):
    key = jax.random.fold_in(key, 7)
    short_key, long_key, jitter_key = jax.random.split(key, 3)
    shorts = jax.random.randint(short_key, (ROWS, SEGS - 1), 1, SHORT_MOST + 1, dtype=jnp.int32)
    chosen = jax.random.randint(long_key, (ROWS, 1), 0, SEGS, dtype=jnp.int32)
    slots = jnp.arange(SEGS, dtype=jnp.int32)[None, :]
    source = jnp.clip(jnp.where(slots < chosen, slots, slots - 1), 0, SEGS - 2)
    picked = jnp.take_along_axis(shorts, jnp.broadcast_to(source, (ROWS, SEGS)), axis=1)
    longest = L - jnp.sum(shorts, axis=1, keepdims=True, dtype=jnp.int32)
    query_rows = jnp.where(slots == chosen, longest, picked).astype(jnp.int32)
    spacing = L // SEGS
    jitter = jax.random.randint(jitter_key, (ROWS, SEGS - 1), 0, max(1, spacing // 2), dtype=jnp.int32)
    base = jnp.arange(1, SEGS, dtype=jnp.int32) * L // SEGS
    inner = base[None, :] + jitter
    begins = jnp.concatenate([jnp.zeros((ROWS, 1), jnp.int32), inner], axis=1)
    ends = jnp.concatenate([inner, jnp.full((ROWS, 1), L, jnp.int32)], axis=1)
    passage_rows = (ends - begins).astype(jnp.int32)
    odd = (jnp.arange(ROWS, dtype=jnp.int32) % 2 == 1)[:, None]
    return jnp.where(odd, passage_rows, query_rows).astype(jnp.int32)


def shard_levels(stream_key, extent, cuts, smallest, high):
    def one(position, parts):
        draws = jax.random.uniform(jax.random.fold_in(jax.random.fold_in(stream_key, 6), position), (parts,), jnp.float32, smallest / len(cuts), high / len(cuts))
        return jnp.repeat(jnp.exp(draws), extent[position] // parts).reshape((-1,) + (1,) * (len(extent) - position - 1))

    level = one(*cuts[0])
    for cut in cuts[1:]:
        level = level * one(*cut)
    return level


def noise(own_key, dims, scale, most, cuts=(), kind=jnp.bfloat16):
    factor_of = shard_levels(own_key, dims, cuts, -0.22, 0.18) if cuts else 1.0
    array = jax.random.normal(own_key, dims, jnp.float32) * scale * factor_of
    return jnp.minimum(jnp.maximum(array, -most), most).astype(kind)


def setup_inputs(seed: int = 0) -> dict:
    key_of = jax.random.split(jax.random.key(seed), 14)
    return {
        "tokens": noise(key_of[0], (ROWS, L, D), 1.0, 6.0, ((0, 8), (1, 4))),
        "lengths": draw_lengths(jax.random.fold_in(key_of[13], 71), 0),
        "positives": jax.random.permutation(key_of[2], NQ).astype(jnp.int32),
        "qkv_weight": noise(key_of[3], (LAYERS, D, 3 * D), D ** -0.5, 0.21875),
        "attn_bias": noise(key_of[4], (LAYERS, 3, D), 0.5, 3.0, (), jnp.float32),
        "out_weight": noise(key_of[5], (LAYERS, D, D), (D // 16) ** -0.5, 0.875),
        "ffn_in": noise(key_of[6], (LAYERS, D, FF), D ** -0.5, 0.21875),
        "ffn_in_bias": noise(key_of[7], (LAYERS, FF), 0.5, 3.0, (), jnp.float32),
        "ffn_out": noise(key_of[8], (LAYERS, FF, D), FF ** -0.5, 0.109375),
        "ffn_out_bias": noise(key_of[9], (LAYERS, D), 0.3, 2.0, (), jnp.float32),
        "norm_gain": jnp.clip(1.0 + 0.1 * jax.random.normal(key_of[10], (LAYERS, 2, D), jnp.float32), 0.5, 1.5),
        "norm_bias": noise(key_of[11], (LAYERS, 2, D), 0.2, 1.5, (), jnp.float32),
        "cotangent": noise(key_of[12], (ROWS, L, D), 1.0, 6.0, ((0, 8), (1, 4))),
    }


EPSILON = 1e-12
NEGATIVE = -1e+30
CONTRAST_WEIGHT = 16.0
HIGHEST = lax.Precision.HIGHEST

@jax.custom_vjp
def low(v):
    return lax.optimization_barrier(v.astype(jnp.bfloat16)).astype(jnp.float32)

@jax.custom_vjp
def low_back(v):
    return v

def low_keep(v):
    return (low(v), None)

def low_pass(kept, grad):
    return (grad,)

def back_keep(v):
    return (v, None)

def back_low(kept, grad):
    return (low(grad),)
low.defvjp(low_keep, low_pass)
low_back.defvjp(back_keep, back_low)

def layout(lengths):
    starts = jnp.cumsum(lengths, axis=1, dtype=jnp.int32) - lengths
    places = jnp.arange(L, dtype=jnp.int32)
    segment = lax.optimization_barrier(jnp.sum((places[None, :, None] >= starts[:, None, 1:]).astype(jnp.int32), axis=2, dtype=jnp.int32))
    return (starts.astype(jnp.int32), segment)

def normalize(hidden, gain, shift):
    centred = hidden - lax.optimization_barrier(jnp.mean(hidden, axis=-1, keepdims=True))
    spread = lax.optimization_barrier(jnp.mean(centred * centred, axis=-1, keepdims=True))
    return centred * lax.rsqrt(spread + EPSILON) * gain + shift

def attention(query, key_block, value_block, segment):
    count = query.shape[0]
    query_heads = query.reshape(count, L, HEADS, HEAD_DIM)
    key_heads = key_block.reshape(count, L, HEADS, HEAD_DIM)
    value_heads = value_block.reshape(count, L, HEADS, HEAD_DIM)
    scaled = jnp.einsum('gqhd,gkhd->ghqk', query_heads, key_heads, precision=HIGHEST) * 0.125
    allowed = segment[:, None, :, None] == segment[:, None, None, :]
    scores = low_back(jnp.where(allowed, scaled, NEGATIVE))
    peak = lax.optimization_barrier(jnp.max(scores, axis=-1, keepdims=True))
    exponent = jnp.exp(scores - peak)
    probability = exponent / lax.optimization_barrier(jnp.sum(exponent, axis=-1, keepdims=True))
    mixed = jnp.einsum('ghqk,gkhd->gqhd', low(probability), value_heads, precision=HIGHEST)
    return mixed.reshape(count, L, D)

def layer(hidden, weights, segment):
    joint_weight, bias_rows, mix_weight, expand_weight, expand_bias, shrink_weight, shrink_bias, gain_rows, shift_rows = weights
    input_low = low(hidden)
    joint = jnp.einsum('gtd,de->gte', input_low, joint_weight, precision=HIGHEST)
    query = low_back(low(joint[..., :D] + bias_rows[0]))
    key_block = low_back(low(joint[..., D:2 * D]))
    value_block = low_back(low(joint[..., 2 * D:] + bias_rows[1]))
    attended = low_back(low(attention(query, key_block, value_block, segment)))
    branch = low_back(jnp.einsum('gtd,de->gte', attended, mix_weight, precision=HIGHEST) + bias_rows[2])
    middle = normalize(hidden + branch, gain_rows[0], shift_rows[0])
    expanded = low_back(jnp.einsum('gtd,df->gtf', low(middle), expand_weight, precision=HIGHEST) + expand_bias)
    active = low(jax.nn.gelu(expanded, approximate=False))
    shrunk = low_back(jnp.einsum('gtf,fd->gtd', active, shrink_weight, precision=HIGHEST) + shrink_bias)
    return normalize(middle + shrunk, gain_rows[1], shift_rows[1])

def forward(hidden, params, lengths, positives):
    starts, segment = layout(lengths)
    count = math.gcd(ROWS, 8)
    grouped = hidden.reshape(ROWS // count, count, L, D)
    grouped_ids = segment.reshape(ROWS // count, count, L)

    def encode(block, block_ids):
        for level in range(LAYERS):
            block = layer(block, tuple((entry[level] for entry in params)), block_ids)
        return block
    encode = jax.checkpoint(encode)

    def advance(carry, item):
        return (carry, encode(item[0], item[1]))
    _, output = lax.scan(advance, jnp.float32(0.0), (grouped, grouped_ids))
    output = output.reshape(ROWS, L, D)
    embedded = low(jnp.take_along_axis(output, starts[:, :, None], axis=1))
    paired = embedded.reshape(ROWS // 2, 2, SEGS, D)
    queries = paired[:, 0].reshape(NQ, D)
    passages = paired[:, 1].reshape(NQ, D)
    contrast = low_back(jnp.dot(queries, passages.T, precision=HIGHEST) * D ** (-0.5))
    peak = lax.optimization_barrier(jnp.max(contrast, axis=1, keepdims=True))
    log_total = peak[:, 0] + jnp.log(lax.optimization_barrier(jnp.sum(jnp.exp(contrast - peak), axis=1)))
    target = jnp.take_along_axis(contrast, positives[:, None], axis=1)[:, 0]
    return (output, jnp.sum(log_total - target))

def reference(tokens, lengths, positives, qkv_weight, attn_bias, out_weight, ffn_in, ffn_in_bias, ffn_out, ffn_out_bias, norm_gain, norm_bias, cotangent):
    params = tuple((entry.astype(jnp.float32) for entry in (qkv_weight, attn_bias, out_weight, ffn_in, ffn_in_bias, ffn_out, ffn_out_bias, norm_gain, norm_bias)))
    hidden = tokens.astype(jnp.float32)

    def objective(start, weights):
        return forward(start, weights, lengths, positives)
    (output, loss), backward = jax.vjp(objective, hidden, params)
    input_grad, grads = backward((cotangent.astype(jnp.float32), jnp.float32(CONTRAST_WEIGHT)))
    return (output.astype(jnp.bfloat16), input_grad, loss, grads[0], grads[1], grads[2], grads[3], grads[4], grads[5], grads[6], grads[7], grads[8])
```

```python
from functools import partial

import jax
import jax.numpy as jnp
from jax import lax
from jax.experimental import pallas as pl
from jax.experimental.pallas import tpu as pltpu
from jax.sharding import PartitionSpec as P

HEADS = 12
HEAD_DIM = 64
PAIR = 2 * HEAD_DIM

EPSILON = 1e-12
NEGATIVE = -1e30
CONTRAST_WEIGHT = 16.0
SCORE_SCALE = 0.125
MIB = 1024 * 1024
VMEM = {
    "attention_forward": 24,
    "shrink_backward": 63,
    "expand_backward": 63,
    "joint_backward": 63,
    "add_blocks": 63,
    "assemble": 56,
    "contrast_part": 56,
}


def cost(microseconds):
    return pl.CostEstimate(
        flops=int(microseconds * 1e9), bytes_accessed=int(microseconds * 2e6), transcendentals=0
    )


GROUPS = (
    ((1, "shrink"), (1, "expand"), (1, "joint")),
    ((0, "shrink"), (0, "expand")),
    ((0, "joint"),),
)

NT = (((1,), (1,)), ((), ()))
TN = (((0,), (0,)), ((), ()))


def dot(a, b, dims=(((1,), (0,)), ((), ()))):
    return lax.dot_general(a, b, dims, preferred_element_type=jnp.float32)


def attention_forward_kernel(step, qkv_ref, column_ids_ref, row_ids_ref, out_ref, lse_ref):
    full_len = qkv_ref.shape[0]
    width = out_ref.shape[1]

    def pair(h, carry):
        offset = pl.multiple_of(h * PAIR, PAIR)
        k = qkv_ref[:, pl.ds(width + offset, PAIR)]
        v_turned = qkv_ref[:, pl.ds(2 * width + offset, PAIR)].T
        for i in range(full_len // step):
            rows = slice(i * step, (i + 1) * step)
            q = qkv_ref[rows, pl.ds(offset, PAIR)]
            q = (q.astype(jnp.float32) * SCORE_SCALE).astype(jnp.bfloat16)
            allowed = column_ids_ref[...] == row_ids_ref[:, rows]
            mixed = []
            for a in range(2):
                cols = slice(a * HEAD_DIM, (a + 1) * HEAD_DIM)
                scores = jnp.where(allowed, dot(k[:, cols], q[:, cols], NT), NEGATIVE)
                peak = jnp.max(scores, axis=0, keepdims=True)
                exponent = jnp.exp(scores - peak)
                summed = jnp.sum(exponent, axis=0, keepdims=True)
                mixed.append(dot(v_turned[cols, :], exponent.astype(jnp.bfloat16)) * (1.0 / summed))
                lse_ref[h, a : a + 1, rows] = peak + jnp.log(summed)
            turned = jnp.concatenate(mixed, axis=0).T
            out_ref[rows, pl.ds(offset, PAIR)] = turned.astype(jnp.bfloat16)
        return carry

    lax.fori_loop(0, width // PAIR, pair, 0)


def attention_forward(qkv, column_ids, row_ids, step):
    full_len = qkv.shape[0]
    width = qkv.shape[1] // 3
    pairs = width // PAIR
    return pl.pallas_call(
        partial(attention_forward_kernel, step),
        out_shape=(
            jax.ShapeDtypeStruct((full_len, width), jnp.bfloat16),
            jax.ShapeDtypeStruct((pairs, 8, full_len), jnp.float32),
        ),
        compiler_params=pltpu.CompilerParams(vmem_limit_bytes=VMEM["attention_forward"] * MIB),
        cost_estimate=cost(8),
    )(qkv, column_ids, row_ids)


def norm_back(grad_out, normed, factor, gain):
    scaled = grad_out * gain
    return factor * (
        scaled
        - jnp.mean(scaled, axis=-1, keepdims=True)
        - normed * jnp.mean(scaled * normed, axis=-1, keepdims=True)
    )


def as_column(row_ref):
    return jnp.broadcast_to(row_ref[...], (128, row_ref.shape[1])).T[:, 0:1]


def store_sums(sums_ref, row, array):
    sums_ref[row : row + 1, :] = jnp.sum(array, axis=0, keepdims=True)


def shrink_backward_kernel(
    shard_columns, bit_ref, grad_ref, normed_ref, factor_ref, gain_ref, active_ref,
    send_ref, keep_ref, sum_grad_ref, low_ref, sums_ref, turned,
):
    @pl.when(pl.program_id(0) == 0)
    def _():
        grad = grad_ref[...]
        normed = normed_ref[...]
        sum_grad = norm_back(grad, normed, as_column(factor_ref), gain_ref[...])
        low = sum_grad.astype(jnp.bfloat16)
        sum_grad_ref[...] = sum_grad
        low_ref[...] = low
        turned[...] = low.T
        sums_ref[...] = jnp.zeros_like(sums_ref)
        store_sums(sums_ref, 0, grad * normed)
        store_sums(sums_ref, 1, grad)
        store_sums(sums_ref, 2, low.astype(jnp.float32))

    half = turned.shape[0] // 2
    bit = bit_ref[0]
    for which, out_ref in ((1 - bit, send_ref), (bit, keep_ref)):
        rows = turned[pl.ds(pl.multiple_of(which * half, half), half), :]
        product = dot(rows, active_ref[...]).astype(jnp.bfloat16)
        if out_ref.shape == product.shape:
            out_ref[...] = product
            continue
        blocks = out_ref.shape[1] // shard_columns
        size = half // blocks
        for shard in range(product.shape[1] // shard_columns):
            columns = slice(shard * shard_columns, (shard + 1) * shard_columns)
            for j in range(blocks):
                out_ref[
                    shard * size : (shard + 1) * size, j * shard_columns : (j + 1) * shard_columns
                ] = product[j * size : (j + 1) * size, columns]


def shrink_backward(bit, grad, normed, factor, gain, active, shards):
    count, width = grad.shape
    inner = active.shape[1]
    steps = inner // width
    shard_columns = inner // shards
    aligned = shard_columns % 128 == 0
    tall, wide = (width, inner // 2) if aligned else (width // 2, inner)
    out_spec = (
        pl.BlockSpec((width // steps, inner // 2), lambda i, bit_ref: (i, 0))
        if aligned
        else pl.BlockSpec((width // 2, width), lambda i, bit_ref: (0, i))
    )

    def whole(*shape):
        return pl.BlockSpec(shape, lambda i, bit_ref: (0, 0))

    send, keep, *others = pl.pallas_call(
        partial(shrink_backward_kernel, shard_columns),
        grid_spec=pltpu.PrefetchScalarGridSpec(
            num_scalar_prefetch=1,
            grid=(steps,),
            in_specs=[
                whole(count, width), whole(count, width), whole(1, count), whole(1, width),
                pl.BlockSpec((count, width), lambda i, bit_ref: (0, i)),
            ],
            out_specs=[
                out_spec, out_spec, whole(count, width), whole(count, width), whole(8, width),
            ],
            scratch_shapes=[pltpu.VMEM((width, count), jnp.bfloat16)],
        ),
        out_shape=[
            jax.ShapeDtypeStruct((tall, wide), jnp.bfloat16),
            jax.ShapeDtypeStruct((tall, wide), jnp.bfloat16),
            jax.ShapeDtypeStruct((count, width), jnp.float32),
            jax.ShapeDtypeStruct((count, width), jnp.bfloat16),
            jax.ShapeDtypeStruct((8, width), jnp.float32),
        ],
        compiler_params=pltpu.CompilerParams(vmem_limit_bytes=VMEM["shrink_backward"] * MIB),
        cost_estimate=cost(6),
    )(bit, grad, normed, factor, gain, active)
    if not aligned:
        shape = (width // 2, shards, shard_columns)
        send, keep = (
            x.reshape(shape).transpose(1, 0, 2).reshape(width, inner // 2) for x in (send, keep)
        )
    return send, keep, *others


def shrink_share(x, shard_columns):
    if shard_columns % 128:
        return x.reshape(-1, shard_columns).T
    size, wide = x.shape
    blocks = wide // shard_columns
    return x.reshape(size, blocks, shard_columns).transpose(2, 1, 0).reshape(shard_columns, -1)


def expand_backward_kernel(
    steps, level, bit_ref, low_ref, sum_grad_ref, slope_ref, middle_ref, shrink_ref, expand_ref,
    normed_ref, factor_ref, gain_ref, mix_ref,
    send_ref, keep_ref, hidden_grad_ref, branch_ref, mixed_grad_ref, sums_ref,
    middle_turned, total, normed_held, sum_grad_held, mix_held, arrived,
):
    step = pl.program_id(0)
    bit = bit_ref[0]
    per_half = steps // 2
    late = (
        pltpu.make_async_copy(normed_ref, normed_held, arrived.at[0]),
        pltpu.make_async_copy(sum_grad_ref, sum_grad_held, arrived.at[1]),
        pltpu.make_async_copy(mix_ref.at[level], mix_held, arrived.at[2]),
    )

    @pl.when(step == 0)
    def _():
        for copy in late:
            copy.start()
        middle_turned[...] = middle_ref[...].T
        total[...] = jnp.zeros_like(total)
        sums_ref[...] = jnp.zeros_like(sums_ref)

    active_grad = dot(low_ref[...], shrink_ref[...], NT)
    expanded = (slope_ref[...].astype(jnp.float32) * active_grad).astype(jnp.bfloat16)
    tile = jnp.where(step < per_half, 1 - bit, bit) * per_half + lax.rem(step, per_half)
    sums_ref[pl.ds(3 + tile, 1), :] = jnp.sum(expanded.astype(jnp.float32), axis=0, keepdims=True)
    weight_grad = dot(middle_turned[...], expanded).astype(jnp.bfloat16)

    @pl.when(step < per_half)
    def _():
        send_ref[...] = weight_grad

    @pl.when(step >= per_half)
    def _():
        keep_ref[...] = weight_grad

    total[...] += dot(expanded, expand_ref[...], NT)

    @pl.when(step == steps - 1)
    def _():
        for copy in late:
            copy.wait()
        grad = total[...] + sum_grad_held[...]
        normed = normed_held[...]
        hidden_grad = norm_back(grad, normed, as_column(factor_ref), gain_ref[...])
        branch = hidden_grad.astype(jnp.bfloat16)
        hidden_grad_ref[...] = hidden_grad
        branch_ref[...] = branch
        store_sums(sums_ref, 0, grad * normed)
        store_sums(sums_ref, 1, grad)
        store_sums(sums_ref, 2, branch.astype(jnp.float32))
        mixed_grad_ref[...] = dot(branch, mix_held[...], NT).astype(jnp.bfloat16)


def expand_backward(
    bit, low, sum_grad, slope, middle, shrink_w, expand_w, normed, factor, gain, mix_w, level
):
    count, width = low.shape
    inner = slope.shape[1]
    steps = inner // width
    per_half = steps // 2

    def whole(*shape):
        return pl.BlockSpec(shape, lambda i, bit_ref: (0, 0))

    anywhere = pl.BlockSpec(memory_space=pl.ANY)

    def tile(i, bit_ref):
        bit = bit_ref[0]
        return jnp.where(i < per_half, 1 - bit, bit) * per_half + lax.rem(i, per_half)

    return pl.pallas_call(
        partial(expand_backward_kernel, steps, level),
        grid_spec=pltpu.PrefetchScalarGridSpec(
            num_scalar_prefetch=1,
            grid=(steps,),
            in_specs=[
                whole(count, width), anywhere,
                pl.BlockSpec((count, width), lambda i, b: (0, tile(i, b))),
                whole(count, width),
                pl.BlockSpec((None, width, width), lambda i, b: (level, tile(i, b), 0)),
                pl.BlockSpec((None, width, width), lambda i, b: (level, 0, tile(i, b))),
                anywhere, whole(1, count), whole(1, width), anywhere,
            ],
            out_specs=[
                pl.BlockSpec((width, width), lambda i, b: (0, jnp.minimum(i, per_half - 1))),
                pl.BlockSpec((width, width), lambda i, b: (0, jnp.maximum(i - per_half, 0))),
                whole(count, width), whole(count, width), whole(count, width), whole(8, width),
            ],
            scratch_shapes=[
                pltpu.VMEM((width, count), jnp.bfloat16),
                pltpu.VMEM((count, width), jnp.float32),
                pltpu.VMEM((count, width), jnp.float32),
                pltpu.VMEM((count, width), jnp.float32),
                pltpu.VMEM((width, width), jnp.bfloat16),
                pltpu.SemaphoreType.DMA((3,)),
            ],
        ),
        out_shape=[
            jax.ShapeDtypeStruct((width, inner // 2), jnp.bfloat16),
            jax.ShapeDtypeStruct((width, inner // 2), jnp.bfloat16),
            jax.ShapeDtypeStruct((count, width), jnp.float32),
            jax.ShapeDtypeStruct((count, width), jnp.bfloat16),
            jax.ShapeDtypeStruct((count, width), jnp.bfloat16),
            jax.ShapeDtypeStruct((8, width), jnp.float32),
        ],
        compiler_params=pltpu.CompilerParams(vmem_limit_bytes=VMEM["expand_backward"] * MIB),
        cost_estimate=cost(16),
    )(bit, low, sum_grad, slope, middle, shrink_w, expand_w, normed, factor, gain, mix_w)


def fetch_all(pairs, semaphores):
    copies = [
        pltpu.make_async_copy(source, target, semaphores.at[i])
        for i, (source, target) in enumerate(pairs)
    ]
    for copy in copies:
        copy.start()
    return copies


def joint_half(half, hidden_ref, mixed_ref, joint_ref, branch_ref, out_ref):
    joint_size, mix_size = joint_ref.shape[1] // 2, branch_ref.shape[1] // 2
    joint = joint_ref[:, pl.ds(pl.multiple_of(half * joint_size, 128), joint_size)]
    branch = branch_ref[:, pl.ds(pl.multiple_of(half * mix_size, 128), mix_size)]
    out_ref[:, :joint_size] = dot(hidden_ref[...].T, joint).astype(jnp.bfloat16)
    out_ref[:, joint_size:] = dot(mixed_ref[...].T, branch).astype(jnp.bfloat16)


def attention_backward_kernel(
    half_ref, lse_ref, column_ids_ref, row_ids_ref, qkv_any, grad_any, mixed_any, hidden_any,
    branch_any, joint_any, half_any, sums_ref,
    qkv_ref, grad_ref, mixed_ref, hidden_ref, branch_ref, joint_ref, out_ref, arrived, left,
):
    fetches = fetch_all(
        (
            (qkv_any, qkv_ref), (grad_any, grad_ref), (mixed_any, mixed_ref),
            (hidden_any, hidden_ref), (branch_any, branch_ref),
        ),
        arrived,
    )
    for fetch in fetches[:3]:
        fetch.wait()
    width = mixed_ref.shape[1]
    lane = lax.broadcasted_iota(jnp.int32, (8, PAIR), 1) // HEAD_DIM
    picker = (lane == lax.broadcasted_iota(jnp.int32, (8, PAIR), 0)).astype(jnp.float32)
    allowed = column_ids_ref[...] == row_ids_ref[...]

    def pair(h, carry):
        offset = pl.multiple_of(h * PAIR, PAIR)
        q = qkv_ref[:, pl.ds(offset, PAIR)]
        k = qkv_ref[:, pl.ds(width + offset, PAIR)]
        v = qkv_ref[:, pl.ds(2 * width + offset, PAIR)]
        grad = grad_ref[:, pl.ds(offset, PAIR)]
        mixed = mixed_ref[:, pl.ds(offset, PAIR)]
        product = grad.astype(jnp.float32) * mixed.astype(jnp.float32)
        centres = lax.dot_general(
            picker, product, NT, precision=lax.Precision.HIGHEST,
            preferred_element_type=jnp.float32,
        )
        q = (q.astype(jnp.float32) * SCORE_SCALE).astype(jnp.bfloat16)
        query_parts, key_parts, value_parts = [], [], []
        for a in range(2):
            cols = slice(a * HEAD_DIM, (a + 1) * HEAD_DIM)
            scores = jnp.where(allowed, dot(k[:, cols], q[:, cols], NT), NEGATIVE)
            probability = jnp.exp(scores - lse_ref[h, a : a + 1, :])
            prob_grad = dot(v[:, cols], grad[:, cols], NT)
            score_low = (probability * (prob_grad - centres[a : a + 1, :])).astype(jnp.bfloat16)
            value_parts.append(dot(probability.astype(jnp.bfloat16), grad[:, cols]))
            key_parts.append(dot(score_low, q[:, cols]))
            query_parts.append(dot(k[:, cols], score_low, TN))
        turned = jnp.concatenate(query_parts, axis=0) * SCORE_SCALE
        for place, part in (
            (0, turned.T),
            (width, jnp.concatenate(key_parts, axis=1)),
            (2 * width, jnp.concatenate(value_parts, axis=1)),
        ):
            joint_ref[:, pl.ds(place + offset, PAIR)] = part.astype(jnp.bfloat16)
        return carry

    lax.fori_loop(0, width // PAIR, pair, 0)
    store_joint = pltpu.make_async_copy(joint_ref, joint_any, left.at[0])
    store_joint.start()
    for fetch in fetches[3:]:
        fetch.wait()
    joint_half(half_ref[0], hidden_ref, mixed_ref, joint_ref, branch_ref, out_ref)
    store_half = pltpu.make_async_copy(out_ref, half_any, left.at[1])
    store_half.start()
    sums_ref[...] = jnp.zeros_like(sums_ref)
    store_sums(sums_ref, 0, joint_ref[:, :width].astype(jnp.float32))
    store_sums(sums_ref, 1, joint_ref[:, 2 * width :].astype(jnp.float32))
    store_joint.wait()
    store_half.wait()


def attention_backward(half, lse, column_ids, row_ids, qkv, grad, mixed, hidden, branch):
    count, width = hidden.shape

    def whole(shape):
        return pl.BlockSpec(shape, lambda i, half_ref: (0,) * len(shape))

    anywhere = pl.BlockSpec(memory_space=pl.ANY)
    return pl.pallas_call(
        attention_backward_kernel,
        grid_spec=pltpu.PrefetchScalarGridSpec(
            num_scalar_prefetch=1,
            grid=(1,),
            in_specs=[whole(lse.shape), whole(column_ids.shape), whole(row_ids.shape)]
            + [anywhere] * 5,
            out_specs=[anywhere] * 2 + [whole((8, width))],
            scratch_shapes=[
                pltpu.VMEM(x.shape, x.dtype) for x in (qkv, grad, mixed, hidden, branch, qkv)
            ]
            + [
                pltpu.VMEM((width, 2 * width), jnp.bfloat16),
                pltpu.SemaphoreType.DMA((5,)),
                pltpu.SemaphoreType.DMA((2,)),
            ],
        ),
        out_shape=[
            low_shape(count, 3 * width),
            low_shape(width, 2 * width),
            jax.ShapeDtypeStruct((8, width), jnp.float32),
        ],
        compiler_params=pltpu.CompilerParams(vmem_limit_bytes=VMEM["joint_backward"] * MIB),
        cost_estimate=cost(14),
    )(half, lse, column_ids, row_ids, qkv, grad, mixed, hidden, branch)


def joint_backward_kernel(
    level, half_ref, mixed_any, hidden_any, joint_any, branch_any, weight_any, hidden_grad_any,
    half_any, out_any,
    mixed_ref, hidden_ref, joint_ref, branch_ref, weight_ref, hidden_grad_ref, part_ref, out_ref,
    arrived, left,
):
    fetches = fetch_all(
        (
            (hidden_any, hidden_ref), (mixed_any, mixed_ref), (joint_any, joint_ref),
            (branch_any, branch_ref), (weight_any.at[level], weight_ref),
            (hidden_grad_any, hidden_grad_ref),
        ),
        arrived,
    )
    for fetch in fetches[:4]:
        fetch.wait()
    joint_half(half_ref[0], hidden_ref, mixed_ref, joint_ref, branch_ref, part_ref)
    store_half = pltpu.make_async_copy(part_ref, half_any, left.at[0])
    store_half.start()
    for fetch in fetches[4:]:
        fetch.wait()
    out_ref[...] = (hidden_grad_ref[...] + dot(joint_ref[...], weight_ref[...], NT)).astype(
        out_ref.dtype
    )
    store_out = pltpu.make_async_copy(out_ref, out_any, left.at[1])
    store_out.start()
    store_half.wait()
    store_out.wait()


def joint_backward(half, mixed, hidden, joint, branch, weight, hidden_grad, level, dtype):
    count, width = hidden.shape
    anywhere = pl.BlockSpec(memory_space=pl.ANY)
    return pl.pallas_call(
        partial(joint_backward_kernel, level),
        grid_spec=pltpu.PrefetchScalarGridSpec(
            num_scalar_prefetch=1,
            grid=(1,),
            in_specs=[anywhere] * 6,
            out_specs=[anywhere] * 2,
            scratch_shapes=[
                pltpu.VMEM(x.shape, x.dtype) for x in (mixed, hidden, joint, branch)
            ]
            + [
                pltpu.VMEM(weight.shape[1:], jnp.bfloat16),
                pltpu.VMEM((count, width), jnp.float32),
                pltpu.VMEM((width, 2 * width), jnp.bfloat16),
                pltpu.VMEM((count, width), dtype),
                pltpu.SemaphoreType.DMA((6,)),
                pltpu.SemaphoreType.DMA((2,)),
            ],
        ),
        out_shape=[low_shape(width, 2 * width), jax.ShapeDtypeStruct((count, width), dtype)],
        compiler_params=pltpu.CompilerParams(vmem_limit_bytes=VMEM["joint_backward"] * MIB),
        cost_estimate=cost(7),
    )(half, mixed, hidden, joint, branch, weight, hidden_grad)


def normalize(hidden):
    centred = hidden - jnp.mean(hidden, axis=-1, keepdims=True)
    spread = jnp.mean(centred * centred, axis=-1, keepdims=True)
    factor = lax.rsqrt(spread + EPSILON)
    return (centred * factor, factor.reshape(1, -1))


def gelu_parts(z):
    phi = 0.5 * (1.0 + lax.erf(z * (0.5**0.5)))
    density = jnp.exp(-0.5 * z * z) * 0.3989422804014327
    return (z * phi, phi + z * density)


def forward_layer(hidden, weights, column_ids, row_ids, step):
    joint_w, bias_rows, mix_w, expand_w, expand_b, shrink_w, shrink_b, gain, shift = weights
    hidden_low = hidden.astype(jnp.bfloat16)
    joint_bias = jnp.concatenate([bias_rows[0], jnp.zeros_like(bias_rows[0]), bias_rows[1]])
    qkv = (dot(hidden_low, joint_w) + joint_bias).astype(jnp.bfloat16)
    mixed, lse = attention_forward(qkv, column_ids, row_ids, step)
    branch = dot(mixed, mix_w) + bias_rows[2]
    normed_one, factor_one = normalize(hidden + branch)
    middle = normed_one * gain[0] + shift[0]
    middle_low = middle.astype(jnp.bfloat16)
    active, slope = gelu_parts(dot(middle_low, expand_w) + expand_b)
    active_low = active.astype(jnp.bfloat16)
    slope = slope.astype(jnp.bfloat16)
    shrunk = dot(active_low, shrink_w) + shrink_b
    normed_two, factor_two = normalize(middle + shrunk)
    result = normed_two * gain[1] + shift[1]
    kept = (
        hidden_low, qkv, lse, mixed, normed_one, factor_one, middle_low, active_low, slope,
        normed_two, factor_two,
    )
    return (result, kept)


def backward_layer(grad, kept, params, column_ids, row_ids, flow, level):
    qkv_weight, out_weight, ffn_in, ffn_out, norm_gain = params
    (
        hidden_low, qkv, lse, mixed, normed_one, factor_one, middle_low, active_low, slope,
        normed_two, factor_two,
    ) = kept
    bit = own_bit("seq", 0).reshape(1)
    send, keep, sum_grad, shrunk_low, sums_two = shrink_backward(
        bit, grad, normed_two, factor_two, norm_gain[level, 1:2], active_low,
        lax.axis_size("batch"),
    )
    shrunk_low, send, keep = flow.tick((shrunk_low, send, keep))
    shrink_keep = keep
    flow.begin((level, "shrink"), reduce_first(send, lambda: shrink_keep, level == 0))
    send, keep, hidden_grad, branch_low, mixed_grad, sums_one = expand_backward(
        bit, shrunk_low, sum_grad, slope, middle_low, ffn_out, ffn_in, normed_one, factor_one,
        norm_gain[level, 0:1], out_weight, level,
    )
    mixed_grad, send, keep = flow.tick((mixed_grad, send, keep))
    expand_keep = keep
    flow.begin((level, "expand"), reduce_first(send, lambda: expand_keep, level == 0))
    joint_low, send, sums_zero = attention_backward(
        1 - bit, lse, column_ids, row_ids, qkv, mixed_grad, mixed, hidden_low, branch_low
    )
    joint_low, send = flow.tick((joint_low, send))
    own_half = Later()
    flow.begin((level, "joint"), reduce_first(send, own_half.get, level == 0))
    own_half.value, input_grad = joint_backward(
        bit, mixed, hidden_low, joint_low, branch_low, qkv_weight, hidden_grad, level,
        jnp.float32 if level else jnp.bfloat16,
    )
    return input_grad, jnp.concatenate([sums_two, sums_one, sums_zero])


def flip(x, axis, bit):
    count = lax.axis_size(axis)
    return lax.ppermute(x, axis, [(i, i ^ (1 << bit)) for i in range(count)])


def own_bit(axis, bit):
    return (lax.axis_index(axis) >> bit) & 1


def add_low(a, b):
    return a + b


def bits_of(axis):
    return (lax.axis_size(axis) - 1).bit_length()


def exchange_rows(pieces):
    count = lax.axis_size("seq")
    own = lax.axis_index("seq")
    arrivals = []
    for k in range(1, count):
        sent = lax.dynamic_index_in_dim(pieces, own ^ k, 0, keepdims=True)
        arrivals.append(lax.ppermute(sent, "seq", [(i, i ^ k) for i in range(count)]))
    arrivals = yield tuple(arrivals)
    result = jnp.zeros_like(pieces)
    mine = lax.dynamic_index_in_dim(pieces, own, 0, keepdims=True)
    result = lax.dynamic_update_slice_in_dim(result, mine, own, 0)
    for k in range(1, count):
        result = lax.dynamic_update_slice_in_dim(result, arrivals[k - 1], own ^ k, 0)
    return result


def swap_rows(pieces):
    return (yield lax.all_to_all(pieces, "seq", 0, 0, tiled=True))


def flip_all(x, mask):
    count = lax.axis_size("batch") * lax.axis_size("seq")
    return lax.ppermute(x, ("batch", "seq"), [(i, i ^ mask) for i in range(count)])


def gather_all(x):
    masks = [0]
    bit = bits_of("batch") + bits_of("seq")
    while bit > 1:
        low = bit - 1
        steps = [m << low for m in range(1 << (bit - low))]
        pieces = [x] + [flip_all(x, m) for m in steps[1:]]
        x = jnp.concatenate(pieces, axis=0)
        masks = [m ^ n for m in steps for n in masks]
        bit = low
    return x, flip_all(x, 1), masks


class Later:
    value = None

    def get(self):
        return self.value


class Flow:
    def __init__(self):
        self.chains = {}
        self.waiting = {}
        self.results = {}

    def begin(self, name, chain):
        self.chains[name] = chain
        self.waiting[name] = next(chain)

    def tick(self, value=()):
        names = list(self.waiting)
        if not names:
            return value
        value, arrived = lax.optimization_barrier((value, [self.waiting[n] for n in names]))
        self.waiting = {}
        for name, array in zip(names, arrived):
            try:
                self.waiting[name] = self.chains[name].send(array)
            except StopIteration as stop:
                self.results[name] = stop.value
        for group in GROUPS:
            if group in self.chains or any(name not in self.results for name in group):
                continue
            chunks = [self.results[name] for name in group]
            self.begin(group, reduce_rest(chunks, group[0][0] == 0, group == GROUPS[-1]))
        return value

    def finish(self):
        while self.waiting:
            self.tick()


def add_blocks_kernel(kernel, counts, bits_ref, *refs):
    ins, outs = counts
    sources, targets = refs[:ins], refs[ins : ins + outs]
    held, made = refs[ins + outs : 2 * ins + outs], refs[2 * ins + outs : 2 * (ins + outs)]
    arrived, left = refs[-2:]
    steps = sources[0].shape[0]
    fetches = [
        [
            pltpu.make_async_copy(source.at[i], target.at[i], arrived.at[j, i])
            for j, (source, target) in enumerate(zip(sources, held))
        ]
        for i in range(steps)
    ]
    for step in fetches:
        for fetch in step:
            fetch.start()
    stores = []
    for i in range(steps):
        for fetch in fetches[i]:
            fetch.wait()
        kernel(bits_ref, *(ref.at[i : i + 1] for ref in (*held, *made)))
        for j, (source, target) in enumerate(zip(made, targets)):
            stores.append(pltpu.make_async_copy(source.at[i], target.at[i], left.at[j, i]))
            stores[-1].start()
    for store in stores:
        store.wait()


def add_blocks(kernel, bits, ins, outs, steps):
    anywhere = pl.BlockSpec(memory_space=pl.ANY)
    return pl.pallas_call(
        partial(add_blocks_kernel, kernel, (len(ins), len(outs))),
        grid_spec=pltpu.PrefetchScalarGridSpec(
            num_scalar_prefetch=1,
            grid=(1,),
            in_specs=[anywhere] * len(ins),
            out_specs=[anywhere] * len(outs),
            scratch_shapes=[pltpu.VMEM(x.shape, jnp.bfloat16) for x in (*ins, *outs)]
            + [
                pltpu.SemaphoreType.DMA((len(ins), steps)),
                pltpu.SemaphoreType.DMA((len(outs), steps)),
            ],
        ),
        out_shape=outs,
        compiler_params=pltpu.CompilerParams(vmem_limit_bytes=VMEM["add_blocks"] * MIB),
        cost_estimate=cost(2),
    )(bits, *ins)


def low_shape(*shape):
    return jax.ShapeDtypeStruct(shape, jnp.bfloat16)


def first_add_kernel(bits_ref, keep_ref, got_ref, send_a, keep_a, send_b, keep_b):
    seq_bit, batch_bit = bits_ref[0], bits_ref[1]
    early = send_a.shape[-1]

    def total(i, j, side):
        columns = slice(early, None) if side else slice(0, early)
        return add_low(keep_ref[o, i, j, :, columns], got_ref[o, i, j, :, columns])

    for o in range(keep_ref.shape[0]):
        for i in range(2):
            send_a[o, i] = total(i, 1 - seq_bit, 0)
            keep_a[o, i] = total(i, seq_bit, 0)
            send_b[o, i] = total(1 - batch_bit, i, 1)
            keep_b[o, i] = total(batch_bit, i, 1)


def second_add_kernel(bits_ref, *refs):
    count = len(refs) // 4 - 1
    outs = refs[4 * count :]
    for chunk in range(count):
        for side in range(2):
            keep_ref, got_ref = refs[4 * chunk + 2 * side : 4 * chunk + 2 * side + 2]
            send_out, keep_out = outs[2 * side : 2 * side + 2]
            bit = bits_ref[1 - side]
            send_out[0, chunk] = add_low(keep_ref[0, 1 - bit], got_ref[0, 1 - bit])
            keep_out[0, chunk] = add_low(keep_ref[0, bit], got_ref[0, bit])


def merge_add_kernel(bits_ref, *refs):
    send_out, keep_out = refs[-2:]
    early = refs[0].shape[-1]
    bit = bits_ref[0]
    place = 0
    for i in range(0, len(refs) - 2, 4):
        chunks = slice(place, place + refs[i].shape[2])
        place = chunks.stop
        for keep_ref, got_ref, columns in (
            (*refs[i : i + 2], slice(0, early)), (*refs[i + 2 : i + 4], slice(early, None)),
        ):
            send_out[0, chunks, :, columns] = add_low(keep_ref[0, 1 - bit], got_ref[0, 1 - bit])
            keep_out[0, chunks, :, columns] = add_low(keep_ref[0, bit], got_ref[0, bit])


def late_add_kernel(bits_ref, keep_ref, got_ref, send_out, keep_out):
    bit = bits_ref[0]
    send_out[0] = add_low(keep_ref[0, 1 - bit], got_ref[0, 1 - bit])
    keep_out[0] = add_low(keep_ref[0, bit], got_ref[0, bit])


def reduce_first(send, get_keep, second=False):
    assert bits_of("seq") == 2
    shards = lax.axis_size("batch")
    rows, columns = send.shape
    outer = shards // 2
    own_rows = rows // shards // 2
    seq_bit, batch_bit = own_bit("seq", 1), own_bit("batch", 0)
    bits = jnp.stack([seq_bit, batch_bit])
    got = yield flip(send, "seq", 0)
    keep = get_keep()
    shape = (outer, 2, 2, own_rows, columns)
    early = columns * 5 // 12
    outs = [low_shape(outer, 2, own_rows, n) for n in (early, early, columns - early, columns - early)]
    send_a, keep_a, send_b, keep_b = add_blocks(
        first_add_kernel, bits, [keep.reshape(shape), got.reshape(shape)], outs, outer
    )
    got_a, got_b = yield (flip(send_a, "seq", 1), flip(send_b, "batch", 0))
    chunk = [keep_a, got_a, keep_b, got_b]
    if second:
        chunk = yield from reduce_second([chunk])
    return chunk


def reduce_second(chunks):
    outer, _, own_rows, early = chunks[0][0].shape
    count = len(chunks)
    late = chunks[0][2].shape[3]
    bits = jnp.stack([own_bit("seq", 1), own_bit("batch", 0)])
    outs = [low_shape(outer, count, own_rows, n) for n in (early, early, late, late)]
    ins = [part for chunk in chunks for part in chunk]
    send_a, keep_a, send_b, keep_b = add_blocks(second_add_kernel, bits, ins, outs, outer)
    got_a, got_b = yield (flip(send_a, "batch", 0), flip(send_b, "seq", 1))
    return [keep_a, got_a, keep_b, got_b]


def reduce_rest(chunks, second, at_once):
    if not second:
        chunks = [(yield from reduce_second(chunks))]
        yield ()
    outer, _, own_rows, early = chunks[0][0].shape
    count = sum(chunk[0].shape[1] for chunk in chunks)
    columns = early + chunks[0][2].shape[3]
    parts = [part for chunk in chunks for part in chunk]
    for bit in range(1, bits_of("batch")):
        outer //= 2
        bits = own_bit("batch", bit).reshape(1)
        ins = [part.reshape((outer, 2) + part.shape[1:]) for part in parts]
        out = low_shape(outer, count, own_rows, columns)
        send, keep = add_blocks(
            merge_add_kernel if bit == 1 else late_add_kernel, bits, ins, [out] * 2, outer
        )
        got = yield flip(send, "batch", bit)
        parts = [keep, got]
    x = add_low(*parts).reshape(count, own_rows, columns)
    if at_once:
        across = lax.ppermute(x, "seq", [(i, i ^ 3) for i in range(lax.axis_size("seq"))])
        got, other, far = yield (flip(x, "seq", 1), flip(x, "seq", 0), across)
        return (x, got), (other, far)
    got = yield flip(x, "seq", 1)
    both = in_order(own_bit("seq", 1), (x, got), 1)
    got = yield flip(both, "seq", 0)
    return both, got


def in_order(bit, pieces, axis):
    own, other = pieces
    upper = bit == 1
    return jnp.concatenate([jnp.where(upper, other, own), jnp.where(upper, own, other)], axis=axis)


def assemble_kernel(
    level_count, shard_columns, bits_ref, tall, tall_got, low, low_got, own, own_got, other,
    other_got, joint_ref, mix_ref, expand_ref, shrink_ref,
):
    core, row_half = bits_ref[0], bits_ref[1]
    joint_size, mix_size = joint_ref.shape[2] // 2, mix_ref.shape[2] // 2
    expand_size = expand_ref.shape[2] // 2
    own_rows = own.shape[1]
    last = level_count - 1

    def columns(side, size):
        return pl.ds(pl.multiple_of(side * size, 128), size)

    def put_shrink(level, value, side):
        blocks = value.shape[1] // shard_columns
        rows = [value[:, j * shard_columns : (j + 1) * shard_columns] for j in range(blocks)]
        turned = jnp.concatenate(rows, axis=0).astype(jnp.float32).T
        shrink_ref[level, :, columns(side, turned.shape[1])] = turned

    def put_expand(level, value, side):
        expand_ref[level, :, columns(side, expand_size)] = value.astype(jnp.float32)

    def put_joint(level, rows, value, side):
        value = value.astype(jnp.float32)
        joint_ref[level, rows, columns(side, joint_size)] = value[:, :joint_size]
        mix_ref[level, rows, columns(side, mix_size)] = value[:, joint_size:]

    for source, partner, side in ((tall, low, core), (tall_got, low_got, 1 - core)):
        put_shrink(last, source[0], side)
        put_expand(last, source[1], side)
        put_joint(last, slice(None), source[2], side)
        put_shrink(0, partner[0], side)
        put_expand(0, partner[1], side)
    for source, half, side in (
        (own, row_half, core), (own_got, 1 - row_half, core),
        (other, row_half, 1 - core), (other_got, 1 - row_half, 1 - core),
    ):
        rows = pl.ds(pl.multiple_of(half * own_rows, own_rows), own_rows)
        put_joint(0, rows, source[0], side)


def assemble(results, level_count, width, inner, shares):
    core, row_half = own_bit("seq", 0), own_bit("seq", 1)
    (tall, tall_got), (low, low_got), last = (results[group] for group in GROUPS)
    (own, own_got), (other, other_got) = last
    rows = width // shares
    shard_columns = inner // shares
    shapes = [
        jax.ShapeDtypeStruct((level_count,) + shape, jnp.float32)
        for shape in ((rows, 3 * width), (rows, width), (rows, inner), (shard_columns, width))
    ]
    if shard_columns % 128 == 0 and rows % 32 == 0:
        return pl.pallas_call(
            partial(assemble_kernel, level_count, shard_columns),
            in_specs=[pl.BlockSpec(memory_space=pltpu.SMEM)]
            + [pl.BlockSpec(memory_space=pltpu.VMEM)] * 8,
            out_shape=shapes,
            compiler_params=pltpu.CompilerParams(vmem_limit_bytes=VMEM["assemble"] * MIB),
            cost_estimate=cost(5),
        )(
            jnp.stack([core, row_half]), tall, tall_got, low, low_got, own, own_got, other,
            other_got,
        )
    joint_size, mix_size = 3 * width // 2, width // 2
    joints = [in_order(row_half, pair, 1)[0] for pair in ((own, own_got), (other, other_got))]
    levels = []
    for shrinks, expands, joints in (
        ((low[0], low_got[0]), (low[1], low_got[1]), joints),
        ((tall[0], tall_got[0]), (tall[1], tall_got[1]), (tall[2], tall_got[2])),
    ):
        levels.append((
            in_order(core, [x[:, :joint_size] for x in joints], 1),
            in_order(core, [x[:, joint_size:] for x in joints], 1),
            in_order(core, expands, 1),
            in_order(core, [shrink_share(x, shard_columns) for x in shrinks], 1),
        ))
    return [jnp.stack(pair).astype(jnp.float32) for pair in zip(*levels)]


def reduce_small(x):
    for axis in ("seq", "batch"):
        for bit in range(bits_of(axis)):
            got = yield flip(x, axis, bit)
            x = x + got
    return x


def contrast_kernel(
    masks, place_ref, starts_ref, same_ref, other_ref, positives_ref, own_cot_ref, *refs
):
    *cot_refs, loss_ref, grad_ref, same, other, rows = refs
    place = place_ref[0]
    pair = place // 2
    seg_count = starts_ref.shape[0]
    width = same_ref.shape[1]
    scale = width ** (-0.5)
    for source, sorted_rows in ((same_ref, same), (other_ref, other)):
        values = source[...].astype(jnp.float32)
        for k, mask in enumerate(masks):
            begin = pl.multiple_of((pair ^ (mask >> 1)) * seg_count, seg_count)
            sorted_rows[pl.ds(begin, seg_count), :] = values[k * seg_count : (k + 1) * seg_count]
    even = place % 2 == 0
    same_rows, other_rows = same[...], other[...]
    queries = jnp.where(even, same_rows, other_rows).astype(jnp.bfloat16)
    passages = jnp.where(even, other_rows, same_rows).astype(jnp.bfloat16)
    contrast = dot(queries, passages, NT) * scale
    peak = jnp.max(contrast, axis=1, keepdims=True)
    log_total = peak + jnp.log(jnp.sum(jnp.exp(contrast - peak), axis=1, keepdims=True))
    turned_hits = positives_ref[...] == lax.broadcasted_iota(jnp.int32, contrast.shape, 0)
    hits = turned_hits.astype(jnp.float32).T
    target = jnp.sum(hits * contrast, axis=1, keepdims=True)
    loss_ref[...] = jnp.sum(log_total - target, axis=0, keepdims=True)
    chance = jnp.exp(contrast - log_total)
    contrast_grad = CONTRAST_WEIGHT * (chance - hits)
    rows[...] = jnp.where(even, contrast_grad, contrast_grad.T)
    begin = pl.multiple_of(pair * seg_count, seg_count)
    own = rows[pl.ds(begin, seg_count), :].astype(jnp.bfloat16)
    owned = dot(own, other_rows.astype(jnp.bfloat16)) * scale
    seq_count, part_len = own_cot_ref.shape[0], own_cot_ref.shape[1]
    at = lax.rem(place, seq_count)
    for k in range(seq_count):
        piece = own_cot_ref[at] if k == 0 else cot_refs[k - 1][0]
        begin = pl.multiple_of((at ^ k) * part_len, part_len)
        grad_ref[pl.ds(begin, part_len), :] = piece.astype(jnp.float32)
    for k in range(seg_count):
        grad_ref[pl.ds(starts_ref[k], 1), :] += owned[k : k + 1, :]


def contrast_part(place, low, starts, positives, cotangent, arrivals):
    full_len, width = low.shape
    seg_count = starts.shape[0]
    places = jnp.arange(full_len, dtype=jnp.int32)
    placed = (starts[:, None] == places[None, :]).astype(jnp.bfloat16)
    picked = dot(placed, low).astype(jnp.bfloat16)
    same, other, masks = gather_all(picked)
    count = same.shape[0]
    ins = [same, other, positives[None, :], cotangent, *arrivals]

    def whole(shape):
        return pl.BlockSpec(shape, lambda i, *_: (0,) * len(shape))

    loss, grad = pl.pallas_call(
        partial(contrast_kernel, masks),
        grid_spec=pltpu.PrefetchScalarGridSpec(
            num_scalar_prefetch=2,
            grid=(1,),
            in_specs=[whole(x.shape) for x in ins],
            out_specs=[whole((1, 1)), whole((full_len, width))],
            scratch_shapes=[
                pltpu.VMEM((count, width), jnp.float32),
                pltpu.VMEM((count, width), jnp.float32),
                pltpu.VMEM((count, count), jnp.float32),
            ],
        ),
        out_shape=[
            jax.ShapeDtypeStruct((1, 1), jnp.float32),
            jax.ShapeDtypeStruct((full_len, width), jnp.float32),
        ],
        compiler_params=pltpu.CompilerParams(vmem_limit_bytes=VMEM["contrast_part"] * MIB),
        cost_estimate=cost(4),
    )(place, starts, *ins)
    return loss[0, 0], grad


def body(
    tokens, lengths, positives, qkv_weight, attn_bias, out_weight, ffn_in, ffn_in_bias, ffn_out,
    ffn_out_bias, norm_gain, norm_bias, cotangent,
):
    batch_rows, part_len, width = tokens.shape
    seq_count = lax.axis_size("seq")
    assert batch_rows == seq_count
    full_len = part_len * seq_count
    own = lax.axis_index("seq")
    own_lengths = lax.dynamic_index_in_dim(lengths, own, 0, keepdims=False)
    starts = jnp.cumsum(own_lengths, dtype=jnp.int32) - own_lengths
    places = jnp.arange(full_len, dtype=jnp.int32)
    segment = jnp.sum(
        (places[:, None] >= starts[None, 1:]).astype(jnp.int32), axis=1, dtype=jnp.int32
    )
    column_ids, row_ids = segment[:, None], segment[None, :]
    params = (
        qkv_weight, attn_bias, out_weight, ffn_in, ffn_in_bias, ffn_out, ffn_out_bias, norm_gain,
        norm_bias,
    )
    level_count = qkv_weight.shape[0]
    flow = Flow()
    flow.begin("tokens", exchange_rows(tokens))
    flow.finish()
    hidden = flow.results["tokens"].reshape(full_len, width).astype(jnp.float32)
    stored = []
    for level in range(level_count):
        weights = tuple(entry[level] for entry in params)
        hidden, kept = forward_layer(hidden, weights, column_ids, row_ids, full_len)
        stored.append(kept)
        if level == 0:
            hidden, cotangent = lax.optimization_barrier((hidden, cotangent))
            arrivals = next(exchange_rows(cotangent))
    low = hidden.astype(jnp.bfloat16)
    place = (lax.axis_index("batch") * seq_count + own).reshape(1)
    loss, grad = contrast_part(place, low, starts, positives, cotangent, arrivals)
    params = (qkv_weight, out_weight, ffn_in, ffn_out, norm_gain)
    sums = [None] * level_count
    for level in reversed(range(level_count)):
        grad, sums[level] = backward_layer(
            grad, stored[level], params, column_ids, row_ids, flow, level
        )
    grad = flow.tick(grad)
    flow.begin("small", reduce_small(jnp.stack(sums)))
    grad = flow.tick(grad)
    flow.begin("input", swap_rows(grad.reshape(batch_rows, part_len, width)))
    flow.tick()
    low = flow.tick(low)
    flow.begin("output", swap_rows(low.reshape(batch_rows, part_len, width)))
    flow.finish()
    layer_output = flow.results["output"]
    returned = flow.results["input"]
    shares = lax.axis_size("batch")
    share = lax.axis_index("batch")
    joint_grad, mix_grad, expand_grad, shrink_grad = assemble(
        flow.results, level_count, width, ffn_in.shape[2], shares
    )
    sums = flow.results["small"]
    inner = ffn_in.shape[2]
    own_sums = lax.dynamic_slice_in_dim(sums, share * (width // shares), width // shares, 2)
    own_inner = lax.dynamic_slice_in_dim(
        sums[:, 11 : 11 + inner // width].reshape(level_count, inner),
        share * (inner // shares), inner // shares, 1,
    )
    bias_grad = jnp.stack([own_sums[:, 16], own_sums[:, 17], own_sums[:, 10]], axis=1)
    expand_bias, shrink_bias = own_inner, own_sums[:, 2]
    gain_grad = jnp.stack([own_sums[:, 8], own_sums[:, 0]], axis=1)
    shift_grad = jnp.stack([own_sums[:, 9], own_sums[:, 1]], axis=1)
    return (
        layer_output, returned.astype(jnp.float32), loss, joint_grad, bias_grad, mix_grad,
        expand_grad, expand_bias, shrink_grad, shrink_bias, gain_grad, shift_grad,
    )


def solution(mesh):
    return jax.shard_map(
        body,
        mesh=mesh,
        in_specs=(
            P("batch", "seq", None), P("batch", None), P(), P(), P(), P(), P(), P(), P(), P(), P(),
            P(), P("batch", "seq", None),
        ),
        out_specs=(
            P("batch", "seq", None),
            P("batch", "seq", None),
            P(),
            P(None, "batch", None),
            P(None, None, "batch"),
            P(None, "batch", None),
            P(None, "batch", None),
            P(None, "batch"),
            P(None, "batch", None),
            P(None, "batch"),
            P(None, None, "batch"),
            P(None, None, "batch"),
        ),
        check_vma=False,
    )
```

```python
from functools import partial

import jax
import jax.numpy as jnp
from jax import lax
from jax.experimental import pallas as pl
from jax.experimental.pallas import tpu as pltpu
from jax.sharding import PartitionSpec as P

HEADS = 12
HEAD_DIM = 64
PAIR = 2 * HEAD_DIM

EPSILON = 1e-12
NEGATIVE = -1e30
CONTRAST_WEIGHT = 16.0
SCORE_SCALE = 0.125
MIB = 1024 * 1024
VMEM = {
    "attention_forward": 24,
    "shrink_backward": 63,
    "expand_backward": 63,
    "joint_backward": 63,
    "add_blocks": 63,
    "assemble": 56,
    "contrast_part": 56,
}


def cost(microseconds):
    return pl.CostEstimate(
        flops=int(microseconds * 1e9), bytes_accessed=int(microseconds * 2e6), transcendentals=0
    )


GROUPS = (
    ((1, "shrink"), (1, "expand"), (1, "joint")),
    ((0, "shrink"), (0, "expand")),
    ((0, "joint"),),
)

NT = (((1,), (1,)), ((), ()))
TN = (((0,), (0,)), ((), ()))


def dot(a, b, dims=(((1,), (0,)), ((), ()))):
    return lax.dot_general(a, b, dims, preferred_element_type=jnp.float32)


def attention_forward_kernel(step, qkv_ref, column_ids_ref, row_ids_ref, out_ref, lse_ref):
    full_len = qkv_ref.shape[0]
    width = out_ref.shape[1]

    def pair(h, carry):
        offset = pl.multiple_of(h * PAIR, PAIR)
        k = qkv_ref[:, pl.ds(width + offset, PAIR)]
        v_turned = qkv_ref[:, pl.ds(2 * width + offset, PAIR)].T
        for i in range(full_len // step):
            rows = slice(i * step, (i + 1) * step)
            q = qkv_ref[rows, pl.ds(offset, PAIR)]
            q = (q.astype(jnp.float32) * SCORE_SCALE).astype(jnp.bfloat16)
            allowed = column_ids_ref[...] == row_ids_ref[:, rows]
            mixed = []
            for a in range(2):
                cols = slice(a * HEAD_DIM, (a + 1) * HEAD_DIM)
                scores = jnp.where(allowed, dot(k[:, cols], q[:, cols], NT), NEGATIVE)
                peak = jnp.max(scores, axis=0, keepdims=True)
                exponent = jnp.exp(scores - peak)
                summed = jnp.sum(exponent, axis=0, keepdims=True)
                mixed.append(dot(v_turned[cols, :], exponent.astype(jnp.bfloat16)) * (1.0 / summed))
                lse_ref[h, a : a + 1, rows] = peak + jnp.log(summed)
            turned = jnp.concatenate(mixed, axis=0).T
            out_ref[rows, pl.ds(offset, PAIR)] = turned.astype(jnp.bfloat16)
        return carry

    lax.fori_loop(0, width // PAIR, pair, 0)


def attention_forward(qkv, column_ids, row_ids, step):
    full_len = qkv.shape[0]
    width = qkv.shape[1] // 3
    pairs = width // PAIR
    return pl.pallas_call(
        partial(attention_forward_kernel, step),
        out_shape=(
            jax.ShapeDtypeStruct((full_len, width), jnp.bfloat16),
            jax.ShapeDtypeStruct((pairs, 8, full_len), jnp.float32),
        ),
        compiler_params=pltpu.CompilerParams(vmem_limit_bytes=VMEM["attention_forward"] * MIB),
        cost_estimate=cost(8),
    )(qkv, column_ids, row_ids)


def norm_back(grad_out, normed, factor, gain):
    scaled = grad_out * gain
    return factor * (
        scaled
        - jnp.mean(scaled, axis=-1, keepdims=True)
        - normed * jnp.mean(scaled * normed, axis=-1, keepdims=True)
    )


def as_column(row_ref):
    return jnp.broadcast_to(row_ref[...], (128, row_ref.shape[1])).T[:, 0:1]


def store_sums(sums_ref, row, array):
    sums_ref[row : row + 1, :] = jnp.sum(array, axis=0, keepdims=True)


def shrink_backward_kernel(
    shard_columns, bit_ref, grad_ref, normed_ref, factor_ref, gain_ref, active_ref,
    send_ref, keep_ref, sum_grad_ref, low_ref, sums_ref, turned,
):
    @pl.when(pl.program_id(0) == 0)
    def _():
        grad = grad_ref[...]
        normed = normed_ref[...]
        sum_grad = norm_back(grad, normed, as_column(factor_ref), gain_ref[...])
        low = sum_grad.astype(jnp.bfloat16)
        sum_grad_ref[...] = sum_grad
        low_ref[...] = low
        turned[...] = low.T
        sums_ref[...] = jnp.zeros_like(sums_ref)
        store_sums(sums_ref, 0, grad * normed)
        store_sums(sums_ref, 1, grad)
        store_sums(sums_ref, 2, low.astype(jnp.float32))

    half = turned.shape[0] // 2
    bit = bit_ref[0]
    for which, out_ref in ((1 - bit, send_ref), (bit, keep_ref)):
        rows = turned[pl.ds(pl.multiple_of(which * half, half), half), :]
        product = dot(rows, active_ref[...]).astype(jnp.bfloat16)
        if out_ref.shape == product.shape:
            out_ref[...] = product
            continue
        blocks = out_ref.shape[1] // shard_columns
        size = half // blocks
        for shard in range(product.shape[1] // shard_columns):
            columns = slice(shard * shard_columns, (shard + 1) * shard_columns)
            for j in range(blocks):
                out_ref[
                    shard * size : (shard + 1) * size, j * shard_columns : (j + 1) * shard_columns
                ] = product[j * size : (j + 1) * size, columns]


def shrink_backward(bit, grad, normed, factor, gain, active, shards):
    count, width = grad.shape
    inner = active.shape[1]
    steps = inner // width
    shard_columns = inner // shards
    aligned = shard_columns % 128 == 0
    tall, wide = (width, inner // 2) if aligned else (width // 2, inner)
    out_spec = (
        pl.BlockSpec((width // steps, inner // 2), lambda i, bit_ref: (i, 0))
        if aligned
        else pl.BlockSpec((width // 2, width), lambda i, bit_ref: (0, i))
    )

    def whole(*shape):
        return pl.BlockSpec(shape, lambda i, bit_ref: (0, 0))

    send, keep, *others = pl.pallas_call(
        partial(shrink_backward_kernel, shard_columns),
        grid_spec=pltpu.PrefetchScalarGridSpec(
            num_scalar_prefetch=1,
            grid=(steps,),
            in_specs=[
                whole(count, width), whole(count, width), whole(1, count), whole(1, width),
                pl.BlockSpec((count, width), lambda i, bit_ref: (0, i)),
            ],
            out_specs=[
                out_spec, out_spec, whole(count, width), whole(count, width), whole(8, width),
            ],
            scratch_shapes=[pltpu.VMEM((width, count), jnp.bfloat16)],
        ),
        out_shape=[
            jax.ShapeDtypeStruct((tall, wide), jnp.bfloat16),
            jax.ShapeDtypeStruct((tall, wide), jnp.bfloat16),
            jax.ShapeDtypeStruct((count, width), jnp.float32),
            jax.ShapeDtypeStruct((count, width), jnp.bfloat16),
            jax.ShapeDtypeStruct((8, width), jnp.float32),
        ],
        compiler_params=pltpu.CompilerParams(vmem_limit_bytes=VMEM["shrink_backward"] * MIB),
        cost_estimate=cost(6),
    )(bit, grad, normed, factor, gain, active)
    if not aligned:
        shape = (width // 2, shards, shard_columns)
        send, keep = (
            x.reshape(shape).transpose(1, 0, 2).reshape(width, inner // 2) for x in (send, keep)
        )
    return send, keep, *others


def shrink_share(x, shard_columns):
    if shard_columns % 128:
        return x.reshape(-1, shard_columns).T
    size, wide = x.shape
    blocks = wide // shard_columns
    return x.reshape(size, blocks, shard_columns).transpose(2, 1, 0).reshape(shard_columns, -1)


def expand_backward_kernel(
    steps, level, bit_ref, low_ref, sum_grad_ref, slope_ref, middle_ref, shrink_ref, expand_ref,
    normed_ref, factor_ref, gain_ref, mix_ref,
    send_ref, keep_ref, hidden_grad_ref, branch_ref, mixed_grad_ref, sums_ref,
    middle_turned, total, normed_held, sum_grad_held, mix_held, arrived,
):
    step = pl.program_id(0)
    bit = bit_ref[0]
    per_half = steps // 2
    late = (
        pltpu.make_async_copy(normed_ref, normed_held, arrived.at[0]),
        pltpu.make_async_copy(sum_grad_ref, sum_grad_held, arrived.at[1]),
        pltpu.make_async_copy(mix_ref.at[level], mix_held, arrived.at[2]),
    )

    @pl.when(step == 0)
    def _():
        for copy in late:
            copy.start()
        middle_turned[...] = middle_ref[...].T
        total[...] = jnp.zeros_like(total)
        sums_ref[...] = jnp.zeros_like(sums_ref)

    active_grad = dot(low_ref[...], shrink_ref[...], NT)
    expanded = (slope_ref[...].astype(jnp.float32) * active_grad).astype(jnp.bfloat16)
    tile = jnp.where(step < per_half, 1 - bit, bit) * per_half + lax.rem(step, per_half)
    sums_ref[pl.ds(3 + tile, 1), :] = jnp.sum(expanded.astype(jnp.float32), axis=0, keepdims=True)
    weight_grad = dot(middle_turned[...], expanded).astype(jnp.bfloat16)

    @pl.when(step < per_half)
    def _():
        send_ref[...] = weight_grad

    @pl.when(step >= per_half)
    def _():
        keep_ref[...] = weight_grad

    total[...] += dot(expanded, expand_ref[...], NT)

    @pl.when(step == steps - 1)
    def _():
        for copy in late:
            copy.wait()
        grad = total[...] + sum_grad_held[...]
        normed = normed_held[...]
        hidden_grad = norm_back(grad, normed, as_column(factor_ref), gain_ref[...])
        branch = hidden_grad.astype(jnp.bfloat16)
        hidden_grad_ref[...] = hidden_grad
        branch_ref[...] = branch
        store_sums(sums_ref, 0, grad * normed)
        store_sums(sums_ref, 1, grad)
        store_sums(sums_ref, 2, branch.astype(jnp.float32))
        mixed_grad_ref[...] = dot(branch, mix_held[...], NT).astype(jnp.bfloat16)


def expand_backward(
    bit, low, sum_grad, slope, middle, shrink_w, expand_w, normed, factor, gain, mix_w, level
):
    count, width = low.shape
    inner = slope.shape[1]
    steps = inner // width
    per_half = steps // 2

    def whole(*shape):
        return pl.BlockSpec(shape, lambda i, bit_ref: (0, 0))

    anywhere = pl.BlockSpec(memory_space=pl.ANY)

    def tile(i, bit_ref):
        bit = bit_ref[0]
        return jnp.where(i < per_half, 1 - bit, bit) * per_half + lax.rem(i, per_half)

    return pl.pallas_call(
        partial(expand_backward_kernel, steps, level),
        grid_spec=pltpu.PrefetchScalarGridSpec(
            num_scalar_prefetch=1,
            grid=(steps,),
            in_specs=[
                whole(count, width), anywhere,
                pl.BlockSpec((count, width), lambda i, b: (0, tile(i, b))),
                whole(count, width),
                pl.BlockSpec((None, width, width), lambda i, b: (level, tile(i, b), 0)),
                pl.BlockSpec((None, width, width), lambda i, b: (level, 0, tile(i, b))),
                anywhere, whole(1, count), whole(1, width), anywhere,
            ],
            out_specs=[
                pl.BlockSpec((width, width), lambda i, b: (0, jnp.minimum(i, per_half - 1))),
                pl.BlockSpec((width, width), lambda i, b: (0, jnp.maximum(i - per_half, 0))),
                whole(count, width), whole(count, width), whole(count, width), whole(8, width),
            ],
            scratch_shapes=[
                pltpu.VMEM((width, count), jnp.bfloat16),
                pltpu.VMEM((count, width), jnp.float32),
                pltpu.VMEM((count, width), jnp.float32),
                pltpu.VMEM((count, width), jnp.float32),
                pltpu.VMEM((width, width), jnp.bfloat16),
                pltpu.SemaphoreType.DMA((3,)),
            ],
        ),
        out_shape=[
            jax.ShapeDtypeStruct((width, inner // 2), jnp.bfloat16),
            jax.ShapeDtypeStruct((width, inner // 2), jnp.bfloat16),
            jax.ShapeDtypeStruct((count, width), jnp.float32),
            jax.ShapeDtypeStruct((count, width), jnp.bfloat16),
            jax.ShapeDtypeStruct((count, width), jnp.bfloat16),
            jax.ShapeDtypeStruct((8, width), jnp.float32),
        ],
        compiler_params=pltpu.CompilerParams(vmem_limit_bytes=VMEM["expand_backward"] * MIB),
        cost_estimate=cost(16),
    )(bit, low, sum_grad, slope, middle, shrink_w, expand_w, normed, factor, gain, mix_w)


def fetch_all(pairs, semaphores):
    copies = [
        pltpu.make_async_copy(source, target, semaphores.at[i])
        for i, (source, target) in enumerate(pairs)
    ]
    for copy in copies:
        copy.start()
    return copies


def joint_half(half, hidden_ref, mixed_ref, joint_ref, branch_ref, out_ref):
    joint_size, mix_size = joint_ref.shape[1] // 2, branch_ref.shape[1] // 2
    joint = joint_ref[:, pl.ds(pl.multiple_of(half * joint_size, 128), joint_size)]
    branch = branch_ref[:, pl.ds(pl.multiple_of(half * mix_size, 128), mix_size)]
    out_ref[:, :joint_size] = dot(hidden_ref[...].T, joint).astype(jnp.bfloat16)
    out_ref[:, joint_size:] = dot(mixed_ref[...].T, branch).astype(jnp.bfloat16)


def attention_backward_kernel(
    half_ref, lse_ref, column_ids_ref, row_ids_ref, qkv_any, grad_any, mixed_any, hidden_any,
    branch_any, joint_any, half_any, sums_ref,
    qkv_ref, grad_ref, mixed_ref, hidden_ref, branch_ref, joint_ref, out_ref, arrived, left,
):
    fetches = fetch_all(
        (
            (qkv_any, qkv_ref), (grad_any, grad_ref), (mixed_any, mixed_ref),
            (hidden_any, hidden_ref), (branch_any, branch_ref),
        ),
        arrived,
    )
    for fetch in fetches[:3]:
        fetch.wait()
    width = mixed_ref.shape[1]
    lane = lax.broadcasted_iota(jnp.int32, (8, PAIR), 1) // HEAD_DIM
    picker = (lane == lax.broadcasted_iota(jnp.int32, (8, PAIR), 0)).astype(jnp.float32)
    allowed = column_ids_ref[...] == row_ids_ref[...]

    def pair(h, carry):
        offset = pl.multiple_of(h * PAIR, PAIR)
        q = qkv_ref[:, pl.ds(offset, PAIR)]
        k = qkv_ref[:, pl.ds(width + offset, PAIR)]
        v = qkv_ref[:, pl.ds(2 * width + offset, PAIR)]
        grad = grad_ref[:, pl.ds(offset, PAIR)]
        mixed = mixed_ref[:, pl.ds(offset, PAIR)]
        product = grad.astype(jnp.float32) * mixed.astype(jnp.float32)
        centres = lax.dot_general(
            picker, product, NT, precision=lax.Precision.HIGHEST,
            preferred_element_type=jnp.float32,
        )
        q = (q.astype(jnp.float32) * SCORE_SCALE).astype(jnp.bfloat16)
        query_parts, key_parts, value_parts = [], [], []
        for a in range(2):
            cols = slice(a * HEAD_DIM, (a + 1) * HEAD_DIM)
            scores = jnp.where(allowed, dot(k[:, cols], q[:, cols], NT), NEGATIVE)
            probability = jnp.exp(scores - lse_ref[h, a : a + 1, :])
            prob_grad = dot(v[:, cols], grad[:, cols], NT)
            score_low = (probability * (prob_grad - centres[a : a + 1, :])).astype(jnp.bfloat16)
            value_parts.append(dot(probability.astype(jnp.bfloat16), grad[:, cols]))
            key_parts.append(dot(score_low, q[:, cols]))
            query_parts.append(dot(k[:, cols], score_low, TN))
        turned = jnp.concatenate(query_parts, axis=0) * SCORE_SCALE
        for place, part in (
            (0, turned.T),
            (width, jnp.concatenate(key_parts, axis=1)),
            (2 * width, jnp.concatenate(value_parts, axis=1)),
        ):
            joint_ref[:, pl.ds(place + offset, PAIR)] = part.astype(jnp.bfloat16)
        return carry

    lax.fori_loop(0, width // PAIR, pair, 0)
    store_joint = pltpu.make_async_copy(joint_ref, joint_any, left.at[0])
    store_joint.start()
    for fetch in fetches[3:]:
        fetch.wait()
    joint_half(half_ref[0], hidden_ref, mixed_ref, joint_ref, branch_ref, out_ref)
    store_half = pltpu.make_async_copy(out_ref, half_any, left.at[1])
    store_half.start()
    sums_ref[...] = jnp.zeros_like(sums_ref)
    store_sums(sums_ref, 0, joint_ref[:, :width].astype(jnp.float32))
    store_sums(sums_ref, 1, joint_ref[:, 2 * width :].astype(jnp.float32))
    store_joint.wait()
    store_half.wait()


def attention_backward(half, lse, column_ids, row_ids, qkv, grad, mixed, hidden, branch):
    count, width = hidden.shape

    def whole(shape):
        return pl.BlockSpec(shape, lambda i, half_ref: (0,) * len(shape))

    anywhere = pl.BlockSpec(memory_space=pl.ANY)
    return pl.pallas_call(
        attention_backward_kernel,
        grid_spec=pltpu.PrefetchScalarGridSpec(
            num_scalar_prefetch=1,
            grid=(1,),
            in_specs=[whole(lse.shape), whole(column_ids.shape), whole(row_ids.shape)]
            + [anywhere] * 5,
            out_specs=[anywhere] * 2 + [whole((8, width))],
            scratch_shapes=[
                pltpu.VMEM(x.shape, x.dtype) for x in (qkv, grad, mixed, hidden, branch, qkv)
            ]
            + [
                pltpu.VMEM((width, 2 * width), jnp.bfloat16),
                pltpu.SemaphoreType.DMA((5,)),
                pltpu.SemaphoreType.DMA((2,)),
            ],
        ),
        out_shape=[
            low_shape(count, 3 * width),
            low_shape(width, 2 * width),
            jax.ShapeDtypeStruct((8, width), jnp.float32),
        ],
        compiler_params=pltpu.CompilerParams(vmem_limit_bytes=VMEM["joint_backward"] * MIB),
        cost_estimate=cost(14),
    )(half, lse, column_ids, row_ids, qkv, grad, mixed, hidden, branch)


def joint_backward_kernel(
    level, half_ref, mixed_any, hidden_any, joint_any, branch_any, weight_any, hidden_grad_any,
    half_any, out_any,
    mixed_ref, hidden_ref, joint_ref, branch_ref, weight_ref, hidden_grad_ref, part_ref, out_ref,
    arrived, left,
):
    fetches = fetch_all(
        (
            (hidden_any, hidden_ref), (mixed_any, mixed_ref), (joint_any, joint_ref),
            (branch_any, branch_ref), (weight_any.at[level], weight_ref),
            (hidden_grad_any, hidden_grad_ref),
        ),
        arrived,
    )
    for fetch in fetches[:4]:
        fetch.wait()
    joint_half(half_ref[0], hidden_ref, mixed_ref, joint_ref, branch_ref, part_ref)
    store_half = pltpu.make_async_copy(part_ref, half_any, left.at[0])
    store_half.start()
    for fetch in fetches[4:]:
        fetch.wait()
    out_ref[...] = (hidden_grad_ref[...] + dot(joint_ref[...], weight_ref[...], NT)).astype(
        out_ref.dtype
    )
    store_out = pltpu.make_async_copy(out_ref, out_any, left.at[1])
    store_out.start()
    store_half.wait()
    store_out.wait()


def joint_backward(half, mixed, hidden, joint, branch, weight, hidden_grad, level, dtype):
    count, width = hidden.shape
    anywhere = pl.BlockSpec(memory_space=pl.ANY)
    return pl.pallas_call(
        partial(joint_backward_kernel, level),
        grid_spec=pltpu.PrefetchScalarGridSpec(
            num_scalar_prefetch=1,
            grid=(1,),
            in_specs=[anywhere] * 6,
            out_specs=[anywhere] * 2,
            scratch_shapes=[
                pltpu.VMEM(x.shape, x.dtype) for x in (mixed, hidden, joint, branch)
            ]
            + [
                pltpu.VMEM(weight.shape[1:], jnp.bfloat16),
                pltpu.VMEM((count, width), jnp.float32),
                pltpu.VMEM((width, 2 * width), jnp.bfloat16),
                pltpu.VMEM((count, width), dtype),
                pltpu.SemaphoreType.DMA((6,)),
                pltpu.SemaphoreType.DMA((2,)),
            ],
        ),
        out_shape=[low_shape(width, 2 * width), jax.ShapeDtypeStruct((count, width), dtype)],
        compiler_params=pltpu.CompilerParams(vmem_limit_bytes=VMEM["joint_backward"] * MIB),
        cost_estimate=cost(7),
    )(half, mixed, hidden, joint, branch, weight, hidden_grad)


def normalize(hidden):
    centred = hidden - jnp.mean(hidden, axis=-1, keepdims=True)
    spread = jnp.mean(centred * centred, axis=-1, keepdims=True)
    factor = lax.rsqrt(spread + EPSILON)
    return (centred * factor, factor.reshape(1, -1))


def gelu_parts(z):
    phi = 0.5 * (1.0 + lax.erf(z * (0.5**0.5)))
    density = jnp.exp(-0.5 * z * z) * 0.3989422804014327
    return (z * phi, phi + z * density)


def forward_layer(hidden, weights, column_ids, row_ids, step):
    joint_w, bias_rows, mix_w, expand_w, expand_b, shrink_w, shrink_b, gain, shift = weights
    hidden_low = hidden.astype(jnp.bfloat16)
    joint_bias = jnp.concatenate([bias_rows[0], jnp.zeros_like(bias_rows[0]), bias_rows[1]])
    qkv = (dot(hidden_low, joint_w) + joint_bias).astype(jnp.bfloat16)
    mixed, lse = attention_forward(qkv, column_ids, row_ids, step)
    branch = dot(mixed, mix_w) + bias_rows[2]
    normed_one, factor_one = normalize(hidden + branch)
    middle = normed_one * gain[0] + shift[0]
    middle_low = middle.astype(jnp.bfloat16)
    active, slope = gelu_parts(dot(middle_low, expand_w) + expand_b)
    active_low = active.astype(jnp.bfloat16)
    slope = slope.astype(jnp.bfloat16)
    shrunk = dot(active_low, shrink_w) + shrink_b
    normed_two, factor_two = normalize(middle + shrunk)
    result = normed_two * gain[1] + shift[1]
    kept = (
        hidden_low, qkv, lse, mixed, normed_one, factor_one, middle_low, active_low, slope,
        normed_two, factor_two,
    )
    return (result, kept)


def backward_layer(grad, kept, params, column_ids, row_ids, flow, level):
    qkv_weight, out_weight, ffn_in, ffn_out, norm_gain = params
    (
        hidden_low, qkv, lse, mixed, normed_one, factor_one, middle_low, active_low, slope,
        normed_two, factor_two,
    ) = kept
    bit = own_bit("seq", 0).reshape(1)
    send, keep, sum_grad, shrunk_low, sums_two = shrink_backward(
        bit, grad, normed_two, factor_two, norm_gain[level, 1:2], active_low,
        lax.axis_size("batch"),
    )
    shrunk_low, send, keep = flow.tick((shrunk_low, send, keep))
    shrink_keep = keep
    flow.begin((level, "shrink"), reduce_first(send, lambda: shrink_keep, level == 0))
    send, keep, hidden_grad, branch_low, mixed_grad, sums_one = expand_backward(
        bit, shrunk_low, sum_grad, slope, middle_low, ffn_out, ffn_in, normed_one, factor_one,
        norm_gain[level, 0:1], out_weight, level,
    )
    mixed_grad, send, keep = flow.tick((mixed_grad, send, keep))
    expand_keep = keep
    flow.begin((level, "expand"), reduce_first(send, lambda: expand_keep, level == 0))
    joint_low, send, sums_zero = attention_backward(
        1 - bit, lse, column_ids, row_ids, qkv, mixed_grad, mixed, hidden_low, branch_low
    )
    joint_low, send = flow.tick((joint_low, send))
    own_half = Later()
    flow.begin((level, "joint"), reduce_first(send, own_half.get, level == 0))
    own_half.value, input_grad = joint_backward(
        bit, mixed, hidden_low, joint_low, branch_low, qkv_weight, hidden_grad, level,
        jnp.float32 if level else jnp.bfloat16,
    )
    return input_grad, jnp.concatenate([sums_two, sums_one, sums_zero])


def flip(x, axis, bit):
    count = lax.axis_size(axis)
    return lax.ppermute(x, axis, [(i, i ^ (1 << bit)) for i in range(count)])


def own_bit(axis, bit):
    return (lax.axis_index(axis) >> bit) & 1


def add_low(a, b):
    return a + b


def bits_of(axis):
    return (lax.axis_size(axis) - 1).bit_length()


def exchange_rows(pieces):
    count = lax.axis_size("seq")
    own = lax.axis_index("seq")
    arrivals = []
    for k in range(1, count):
        sent = lax.dynamic_index_in_dim(pieces, own ^ k, 0, keepdims=True)
        arrivals.append(lax.ppermute(sent, "seq", [(i, i ^ k) for i in range(count)]))
    arrivals = yield tuple(arrivals)
    result = jnp.zeros_like(pieces)
    mine = lax.dynamic_index_in_dim(pieces, own, 0, keepdims=True)
    result = lax.dynamic_update_slice_in_dim(result, mine, own, 0)
    for k in range(1, count):
        result = lax.dynamic_update_slice_in_dim(result, arrivals[k - 1], own ^ k, 0)
    return result


def swap_rows(pieces):
    return (yield lax.all_to_all(pieces, "seq", 0, 0, tiled=True))


def flip_all(x, mask):
    count = lax.axis_size("batch") * lax.axis_size("seq")
    return lax.ppermute(x, ("batch", "seq"), [(i, i ^ mask) for i in range(count)])


def gather_all(x):
    masks = [0]
    bit = bits_of("batch") + bits_of("seq")
    while bit > 1:
        low = bit - 1
        steps = [m << low for m in range(1 << (bit - low))]
        pieces = [x] + [flip_all(x, m) for m in steps[1:]]
        x = jnp.concatenate(pieces, axis=0)
        masks = [m ^ n for m in steps for n in masks]
        bit = low
    return x, flip_all(x, 1), masks


class Later:
    value = None

    def get(self):
        return self.value


class Flow:
    def __init__(self):
        self.chains = {}
        self.waiting = {}
        self.results = {}

    def begin(self, name, chain):
        self.chains[name] = chain
        self.waiting[name] = next(chain)

    def tick(self, value=()):
        names = list(self.waiting)
        if not names:
            return value
        value, arrived = lax.optimization_barrier((value, [self.waiting[n] for n in names]))
        self.waiting = {}
        for name, array in zip(names, arrived):
            try:
                self.waiting[name] = self.chains[name].send(array)
            except StopIteration as stop:
                self.results[name] = stop.value
        for group in GROUPS:
            if group in self.chains or any(name not in self.results for name in group):
                continue
            chunks = [self.results[name] for name in group]
            self.begin(group, reduce_rest(chunks, group[0][0] == 0, group == GROUPS[-1]))
        return value

    def finish(self):
        while self.waiting:
            self.tick()


def add_blocks_kernel(kernel, counts, bits_ref, *refs):
    ins, outs = counts
    sources, targets = refs[:ins], refs[ins : ins + outs]
    held, made = refs[ins + outs : 2 * ins + outs], refs[2 * ins + outs : 2 * (ins + outs)]
    arrived, left = refs[-2:]
    steps = sources[0].shape[0]
    fetches = [
        [
            pltpu.make_async_copy(source.at[i], target.at[i], arrived.at[j, i])
            for j, (source, target) in enumerate(zip(sources, held))
        ]
        for i in range(steps)
    ]
    for step in fetches:
        for fetch in step:
            fetch.start()
    stores = []
    for i in range(steps):
        for fetch in fetches[i]:
            fetch.wait()
        kernel(bits_ref, *(ref.at[i : i + 1] for ref in (*held, *made)))
        for j, (source, target) in enumerate(zip(made, targets)):
            stores.append(pltpu.make_async_copy(source.at[i], target.at[i], left.at[j, i]))
            stores[-1].start()
    for store in stores:
        store.wait()


def add_blocks(kernel, bits, ins, outs, steps):
    anywhere = pl.BlockSpec(memory_space=pl.ANY)
    return pl.pallas_call(
        partial(add_blocks_kernel, kernel, (len(ins), len(outs))),
        grid_spec=pltpu.PrefetchScalarGridSpec(
            num_scalar_prefetch=1,
            grid=(1,),
            in_specs=[anywhere] * len(ins),
            out_specs=[anywhere] * len(outs),
            scratch_shapes=[pltpu.VMEM(x.shape, jnp.bfloat16) for x in (*ins, *outs)]
            + [
                pltpu.SemaphoreType.DMA((len(ins), steps)),
                pltpu.SemaphoreType.DMA((len(outs), steps)),
            ],
        ),
        out_shape=outs,
        compiler_params=pltpu.CompilerParams(vmem_limit_bytes=VMEM["add_blocks"] * MIB),
        cost_estimate=cost(2),
    )(bits, *ins)


def low_shape(*shape):
    return jax.ShapeDtypeStruct(shape, jnp.bfloat16)


def first_add_kernel(bits_ref, keep_ref, got_ref, send_a, keep_a, send_b, keep_b):
    seq_bit, batch_bit = bits_ref[0], bits_ref[1]
    early = send_a.shape[-1]

    def total(i, j, side):
        columns = slice(early, None) if side else slice(0, early)
        return add_low(keep_ref[o, i, j, :, columns], got_ref[o, i, j, :, columns])

    for o in range(keep_ref.shape[0]):
        for i in range(2):
            send_a[o, i] = total(i, 1 - seq_bit, 0)
            keep_a[o, i] = total(i, seq_bit, 0)
            send_b[o, i] = total(1 - batch_bit, i, 1)
            keep_b[o, i] = total(batch_bit, i, 1)


def second_add_kernel(bits_ref, *refs):
    count = len(refs) // 4 - 1
    outs = refs[4 * count :]
    for chunk in range(count):
        for side in range(2):
            keep_ref, got_ref = refs[4 * chunk + 2 * side : 4 * chunk + 2 * side + 2]
            send_out, keep_out = outs[2 * side : 2 * side + 2]
            bit = bits_ref[1 - side]
            send_out[0, chunk] = add_low(keep_ref[0, 1 - bit], got_ref[0, 1 - bit])
            keep_out[0, chunk] = add_low(keep_ref[0, bit], got_ref[0, bit])


def merge_add_kernel(bits_ref, *refs):
    send_out, keep_out = refs[-2:]
    early = refs[0].shape[-1]
    bit = bits_ref[0]
    place = 0
    for i in range(0, len(refs) - 2, 4):
        chunks = slice(place, place + refs[i].shape[2])
        place = chunks.stop
        for keep_ref, got_ref, columns in (
            (*refs[i : i + 2], slice(0, early)), (*refs[i + 2 : i + 4], slice(early, None)),
        ):
            send_out[0, chunks, :, columns] = add_low(keep_ref[0, 1 - bit], got_ref[0, 1 - bit])
            keep_out[0, chunks, :, columns] = add_low(keep_ref[0, bit], got_ref[0, bit])


def late_add_kernel(bits_ref, keep_ref, got_ref, send_out, keep_out):
    bit = bits_ref[0]
    send_out[0] = add_low(keep_ref[0, 1 - bit], got_ref[0, 1 - bit])
    keep_out[0] = add_low(keep_ref[0, bit], got_ref[0, bit])


def reduce_first(send, get_keep, second=False):
    assert bits_of("seq") == 2
    shards = lax.axis_size("batch")
    rows, columns = send.shape
    outer = shards // 2
    own_rows = rows // shards // 2
    seq_bit, batch_bit = own_bit("seq", 1), own_bit("batch", 0)
    bits = jnp.stack([seq_bit, batch_bit])
    got = yield flip(send, "seq", 0)
    keep = get_keep()
    shape = (outer, 2, 2, own_rows, columns)
    early = columns * 5 // 12
    outs = [low_shape(outer, 2, own_rows, n) for n in (early, early, columns - early, columns - early)]
    send_a, keep_a, send_b, keep_b = add_blocks(
        first_add_kernel, bits, [keep.reshape(shape), got.reshape(shape)], outs, outer
    )
    got_a, got_b = yield (flip(send_a, "seq", 1), flip(send_b, "batch", 0))
    chunk = [keep_a, got_a, keep_b, got_b]
    if second:
        chunk = yield from reduce_second([chunk])
    return chunk


def reduce_second(chunks):
    outer, _, own_rows, early = chunks[0][0].shape
    count = len(chunks)
    late = chunks[0][2].shape[3]
    bits = jnp.stack([own_bit("seq", 1), own_bit("batch", 0)])
    outs = [low_shape(outer, count, own_rows, n) for n in (early, early, late, late)]
    ins = [part for chunk in chunks for part in chunk]
    send_a, keep_a, send_b, keep_b = add_blocks(second_add_kernel, bits, ins, outs, outer)
    got_a, got_b = yield (flip(send_a, "batch", 0), flip(send_b, "seq", 1))
    return [keep_a, got_a, keep_b, got_b]


def reduce_rest(chunks, second, at_once):
    if not second:
        chunks = [(yield from reduce_second(chunks))]
        yield ()
    outer, _, own_rows, early = chunks[0][0].shape
    count = sum(chunk[0].shape[1] for chunk in chunks)
    columns = early + chunks[0][2].shape[3]
    parts = [part for chunk in chunks for part in chunk]
    for bit in range(1, bits_of("batch")):
        outer //= 2
        bits = own_bit("batch", bit).reshape(1)
        ins = [part.reshape((outer, 2) + part.shape[1:]) for part in parts]
        out = low_shape(outer, count, own_rows, columns)
        send, keep = add_blocks(
            merge_add_kernel if bit == 1 else late_add_kernel, bits, ins, [out] * 2, outer
        )
        got = yield flip(send, "batch", bit)
        parts = [keep, got]
    x = add_low(*parts).reshape(count, own_rows, columns)
    if at_once:
        across = lax.ppermute(x, "seq", [(i, i ^ 3) for i in range(lax.axis_size("seq"))])
        got, other, far = yield (flip(x, "seq", 1), flip(x, "seq", 0), across)
        return (x, got), (other, far)
    got = yield flip(x, "seq", 1)
    both = in_order(own_bit("seq", 1), (x, got), 1)
    got = yield flip(both, "seq", 0)
    return both, got


def in_order(bit, pieces, axis):
    own, other = pieces
    upper = bit == 1
    return jnp.concatenate([jnp.where(upper, other, own), jnp.where(upper, own, other)], axis=axis)


def assemble_kernel(
    level_count, shard_columns, bits_ref, tall, tall_got, low, low_got, own, own_got, other,
    other_got, joint_ref, mix_ref, expand_ref, shrink_ref,
):
    core, row_half = bits_ref[0], bits_ref[1]
    joint_size, mix_size = joint_ref.shape[2] // 2, mix_ref.shape[2] // 2
    expand_size = expand_ref.shape[2] // 2
    own_rows = own.shape[1]
    last = level_count - 1

    def columns(side, size):
        return pl.ds(pl.multiple_of(side * size, 128), size)

    def put_shrink(level, value, side):
        blocks = value.shape[1] // shard_columns
        rows = [value[:, j * shard_columns : (j + 1) * shard_columns] for j in range(blocks)]
        turned = jnp.concatenate(rows, axis=0).astype(jnp.float32).T
        shrink_ref[level, :, columns(side, turned.shape[1])] = turned

    def put_expand(level, value, side):
        expand_ref[level, :, columns(side, expand_size)] = value.astype(jnp.float32)

    def put_joint(level, rows, value, side):
        value = value.astype(jnp.float32)
        joint_ref[level, rows, columns(side, joint_size)] = value[:, :joint_size]
        mix_ref[level, rows, columns(side, mix_size)] = value[:, joint_size:]

    for source, partner, side in ((tall, low, core), (tall_got, low_got, 1 - core)):
        put_shrink(last, source[0], side)
        put_expand(last, source[1], side)
        put_joint(last, slice(None), source[2], side)
        put_shrink(0, partner[0], side)
        put_expand(0, partner[1], side)
    for source, half, side in (
        (own, row_half, core), (own_got, 1 - row_half, core),
        (other, row_half, 1 - core), (other_got, 1 - row_half, 1 - core),
    ):
        rows = pl.ds(pl.multiple_of(half * own_rows, own_rows), own_rows)
        put_joint(0, rows, source[0], side)


def assemble(results, level_count, width, inner, shares):
    core, row_half = own_bit("seq", 0), own_bit("seq", 1)
    (tall, tall_got), (low, low_got), last = (results[group] for group in GROUPS)
    (own, own_got), (other, other_got) = last
    rows = width // shares
    shard_columns = inner // shares
    shapes = [
        jax.ShapeDtypeStruct((level_count,) + shape, jnp.float32)
        for shape in ((rows, 3 * width), (rows, width), (rows, inner), (shard_columns, width))
    ]
    if shard_columns % 128 == 0 and rows % 32 == 0:
        return pl.pallas_call(
            partial(assemble_kernel, level_count, shard_columns),
            in_specs=[pl.BlockSpec(memory_space=pltpu.SMEM)]
            + [pl.BlockSpec(memory_space=pltpu.VMEM)] * 8,
            out_shape=shapes,
            compiler_params=pltpu.CompilerParams(vmem_limit_bytes=VMEM["assemble"] * MIB),
            cost_estimate=cost(5),
        )(
            jnp.stack([core, row_half]), tall, tall_got, low, low_got, own, own_got, other,
            other_got,
        )
    joint_size, mix_size = 3 * width // 2, width // 2
    joints = [in_order(row_half, pair, 1)[0] for pair in ((own, own_got), (other, other_got))]
    levels = []
    for shrinks, expands, joints in (
        ((low[0], low_got[0]), (low[1], low_got[1]), joints),
        ((tall[0], tall_got[0]), (tall[1], tall_got[1]), (tall[2], tall_got[2])),
    ):
        levels.append((
            in_order(core, [x[:, :joint_size] for x in joints], 1),
            in_order(core, [x[:, joint_size:] for x in joints], 1),
            in_order(core, expands, 1),
            in_order(core, [shrink_share(x, shard_columns) for x in shrinks], 1),
        ))
    return [jnp.stack(pair).astype(jnp.float32) for pair in zip(*levels)]


def reduce_small(x):
    for axis in ("seq", "batch"):
        for bit in range(bits_of(axis)):
            got = yield flip(x, axis, bit)
            x = x + got
    return x


def contrast_kernel(
    masks, place_ref, starts_ref, same_ref, other_ref, positives_ref, own_cot_ref, *refs
):
    *cot_refs, loss_ref, grad_ref, same, other, rows = refs
    place = place_ref[0]
    pair = place // 2
    seg_count = starts_ref.shape[0]
    width = same_ref.shape[1]
    scale = width ** (-0.5)
    for source, sorted_rows in ((same_ref, same), (other_ref, other)):
        values = source[...].astype(jnp.float32)
        for k, mask in enumerate(masks):
            begin = pl.multiple_of((pair ^ (mask >> 1)) * seg_count, seg_count)
            sorted_rows[pl.ds(begin, seg_count), :] = values[k * seg_count : (k + 1) * seg_count]
    even = place % 2 == 0
    same_rows, other_rows = same[...], other[...]
    queries = jnp.where(even, same_rows, other_rows).astype(jnp.bfloat16)
    passages = jnp.where(even, other_rows, same_rows).astype(jnp.bfloat16)
    contrast = dot(queries, passages, NT) * scale
    peak = jnp.max(contrast, axis=1, keepdims=True)
    log_total = peak + jnp.log(jnp.sum(jnp.exp(contrast - peak), axis=1, keepdims=True))
    turned_hits = positives_ref[...] == lax.broadcasted_iota(jnp.int32, contrast.shape, 0)
    hits = turned_hits.astype(jnp.float32).T
    target = jnp.sum(hits * contrast, axis=1, keepdims=True)
    loss_ref[...] = jnp.sum(log_total - target, axis=0, keepdims=True)
    chance = jnp.exp(contrast - log_total)
    contrast_grad = CONTRAST_WEIGHT * (chance - hits)
    rows[...] = jnp.where(even, contrast_grad, contrast_grad.T)
    begin = pl.multiple_of(pair * seg_count, seg_count)
    own = rows[pl.ds(begin, seg_count), :].astype(jnp.bfloat16)
    owned = dot(own, other_rows.astype(jnp.bfloat16)) * scale
    seq_count, part_len = own_cot_ref.shape[0], own_cot_ref.shape[1]
    at = lax.rem(place, seq_count)
    for k in range(seq_count):
        piece = own_cot_ref[at] if k == 0 else cot_refs[k - 1][0]
        begin = pl.multiple_of((at ^ k) * part_len, part_len)
        grad_ref[pl.ds(begin, part_len), :] = piece.astype(jnp.float32)
    for k in range(seg_count):
        grad_ref[pl.ds(starts_ref[k], 1), :] += owned[k : k + 1, :]


def contrast_part(place, low, starts, positives, cotangent, arrivals):
    full_len, width = low.shape
    seg_count = starts.shape[0]
    places = jnp.arange(full_len, dtype=jnp.int32)
    placed = (starts[:, None] == places[None, :]).astype(jnp.bfloat16)
    picked = dot(placed, low).astype(jnp.bfloat16)
    same, other, masks = gather_all(picked)
    count = same.shape[0]
    ins = [same, other, positives[None, :], cotangent, *arrivals]

    def whole(shape):
        return pl.BlockSpec(shape, lambda i, *_: (0,) * len(shape))

    loss, grad = pl.pallas_call(
        partial(contrast_kernel, masks),
        grid_spec=pltpu.PrefetchScalarGridSpec(
            num_scalar_prefetch=2,
            grid=(1,),
            in_specs=[whole(x.shape) for x in ins],
            out_specs=[whole((1, 1)), whole((full_len, width))],
            scratch_shapes=[
                pltpu.VMEM((count, width), jnp.float32),
                pltpu.VMEM((count, width), jnp.float32),
                pltpu.VMEM((count, count), jnp.float32),
            ],
        ),
        out_shape=[
            jax.ShapeDtypeStruct((1, 1), jnp.float32),
            jax.ShapeDtypeStruct((full_len, width), jnp.float32),
        ],
        compiler_params=pltpu.CompilerParams(vmem_limit_bytes=VMEM["contrast_part"] * MIB),
        cost_estimate=cost(4),
    )(place, starts, *ins)
    return loss[0, 0], grad


def body(
    tokens, lengths, positives, qkv_weight, attn_bias, out_weight, ffn_in, ffn_in_bias, ffn_out,
    ffn_out_bias, norm_gain, norm_bias, cotangent,
):
    batch_rows, part_len, width = tokens.shape
    seq_count = lax.axis_size("seq")
    assert batch_rows == seq_count
    full_len = part_len * seq_count
    own = lax.axis_index("seq")
    own_lengths = lax.dynamic_index_in_dim(lengths, own, 0, keepdims=False)
    starts = jnp.cumsum(own_lengths, dtype=jnp.int32) - own_lengths
    places = jnp.arange(full_len, dtype=jnp.int32)
    segment = jnp.sum(
        (places[:, None] >= starts[None, 1:]).astype(jnp.int32), axis=1, dtype=jnp.int32
    )
    column_ids, row_ids = segment[:, None], segment[None, :]
    params = (
        qkv_weight, attn_bias, out_weight, ffn_in, ffn_in_bias, ffn_out, ffn_out_bias, norm_gain,
        norm_bias,
    )
    level_count = qkv_weight.shape[0]
    flow = Flow()
    flow.begin("tokens", exchange_rows(tokens))
    flow.finish()
    hidden = flow.results["tokens"].reshape(full_len, width).astype(jnp.float32)
    stored = []
    for level in range(level_count):
        weights = tuple(entry[level] for entry in params)
        hidden, kept = forward_layer(hidden, weights, column_ids, row_ids, full_len)
        stored.append(kept)
        if level == 0:
            hidden, cotangent = lax.optimization_barrier((hidden, cotangent))
            arrivals = next(exchange_rows(cotangent))
    low = hidden.astype(jnp.bfloat16)
    place = (lax.axis_index("batch") * seq_count + own).reshape(1)
    loss, grad = contrast_part(place, low, starts, positives, cotangent, arrivals)
    params = (qkv_weight, out_weight, ffn_in, ffn_out, norm_gain)
    sums = [None] * level_count
    for level in reversed(range(level_count)):
        grad, sums[level] = backward_layer(
            grad, stored[level], params, column_ids, row_ids, flow, level
        )
    grad = flow.tick(grad)
    flow.begin("small", reduce_small(jnp.stack(sums)))
    grad = flow.tick(grad)
    pieces = [x.reshape(batch_rows, part_len, width) for x in (low, grad)]
    flow.begin("rows", swap_rows(jnp.stack(pieces, axis=1)))
    flow.finish()
    layer_output, returned = (flow.results["rows"][:, i] for i in range(2))
    shares = lax.axis_size("batch")
    share = lax.axis_index("batch")
    joint_grad, mix_grad, expand_grad, shrink_grad = assemble(
        flow.results, level_count, width, ffn_in.shape[2], shares
    )
    sums = flow.results["small"]
    inner = ffn_in.shape[2]
    own_sums = lax.dynamic_slice_in_dim(sums, share * (width // shares), width // shares, 2)
    own_inner = lax.dynamic_slice_in_dim(
        sums[:, 11 : 11 + inner // width].reshape(level_count, inner),
        share * (inner // shares), inner // shares, 1,
    )
    bias_grad = jnp.stack([own_sums[:, 16], own_sums[:, 17], own_sums[:, 10]], axis=1)
    expand_bias, shrink_bias = own_inner, own_sums[:, 2]
    gain_grad = jnp.stack([own_sums[:, 8], own_sums[:, 0]], axis=1)
    shift_grad = jnp.stack([own_sums[:, 9], own_sums[:, 1]], axis=1)
    return (
        layer_output, returned.astype(jnp.float32), loss, joint_grad, bias_grad, mix_grad,
        expand_grad, expand_bias, shrink_grad, shrink_bias, gain_grad, shift_grad,
    )


def solution(mesh):
    return jax.shard_map(
        body,
        mesh=mesh,
        in_specs=(
            P("batch", "seq", None), P("batch", None), P(), P(), P(), P(), P(), P(), P(), P(), P(),
            P(), P("batch", "seq", None),
        ),
        out_specs=(
            P("batch", "seq", None),
            P("batch", "seq", None),
            P(),
            P(None, "batch", None),
            P(None, None, "batch"),
            P(None, "batch", None),
            P(None, "batch", None),
            P(None, "batch"),
            P(None, "batch", None),
            P(None, "batch"),
            P(None, None, "batch"),
            P(None, None, "batch"),
        ),
        check_vma=False,
    )
```
